128 devices in a mesh: row: 8 (over z, core), col: 16 (over y, x).
Axes of the slice: x: 4, y: 4, z: 4, core: 2. Of those that a mesh axis runs over, the one named last changes fastest.
Arguments:
- image: float32 [32, 32, 64, 128], P('row', 'col'), may hold values from -6 to 6
- u_factors: bfloat16 [40, 64, 1024, 256], P('row', 'col'), may hold values from -0.0625 to 0.0625
- v_factors: bfloat16 [40, 64, 1024, 256], P('row', 'col'), may hold values from -0.1875 to 0.1875
- ranks: int32 [40, 64], P('row', 'col'), may hold values from 16 to 256
- measured: bfloat16 [40960, 128], P('row'), may hold values from -6 to 6
Outputs:
- new_image: float32 [32, 32, 64, 128], P('row', 'col')
The draws below stay inside these ranges and needn't reach their ends.
All inputs are finite; a program needn't handle non-finite values.
Results may differ from the reference program's by a relative error of at most 0.0051.
Values may be sent and summed in bfloat16 or wider, within the bound.
A program may use at most 128 MiB of HBM per device.

```python
import jax
import jax.numpy as jnp
from jax import lax

TILE = 1024
RMAX = 256
F = 128
GZ = 64
GX = 32
GY = 32
COL_TILES = 64
ROW_TILES = 40
SAMPLES = 40960
N_COL = 16


def touch_ends(drawn, own_key, least, largest):
    longest = drawn.shape.index(max(drawn.shape))
    spots = []
    for shift in (0, 1):
        where = [jax.random.randint(jax.random.fold_in(own_key, axis), (), 0, length) for axis, length in enumerate(drawn.shape)]
        where[longest] = (where[longest] + shift) % drawn.shape[longest]
        spots.append(tuple(where))
    return drawn.at[spots[0]].set(least).at[spots[1]].set(largest)


def shard_levels(stream_key, extent, pieces, smallest, top_value):
    gain = 1.0
    for position, shards_of in pieces:
        steps = jax.random.uniform(jax.random.fold_in(jax.random.fold_in(stream_key, 6), position), (shards_of,), jnp.float32, smallest / len(pieces), top_value / len(pieces))
        gain = gain * jnp.repeat(jnp.exp(steps), extent[position] // shards_of).reshape((-1,) + (1,) * (len(extent) - 1 - position))
    return gain


def bell_draw(key, extent, scale, bound, cuts=(), kind=jnp.bfloat16):
    drawn = jax.random.normal(key, extent, jnp.float32) * scale
    if len(cuts) > 0:
        drawn = shard_levels(key, extent, cuts, -0.22, 0.18) * drawn
    return jnp.clip(drawn, min=-bound, max=bound).astype(kind)


def setup_inputs(seed: int = 0) -> dict:
    key_of = jax.random.split(jax.random.key(seed), 6)
    return {
        "image": bell_draw(key_of[0], (GX, GY, GZ, F), 1.0, 6.0, ((0, 8), (1, 16)), jnp.float32),
        "u_factors": bell_draw(key_of[1], (ROW_TILES, COL_TILES, TILE, RMAX), (RMAX * COL_TILES // 2) ** -0.5, 0.0625, ((0, 8), (1, 16))),
        "v_factors": bell_draw(key_of[2], (ROW_TILES, COL_TILES, TILE, RMAX), TILE ** -0.5, 0.1875, ((0, 8), (1, 16))),
        "ranks": touch_ends(jax.random.randint(key_of[3], (ROW_TILES, COL_TILES), RMAX // 16, RMAX + 1), jax.random.fold_in(key_of[3], 1), RMAX // 16, RMAX).astype(jnp.int32),
        "measured": bell_draw(key_of[4], (SAMPLES, F), 1.0, 6.0, ((0, 8),)),
    }


diff_rate = 0.12
edge_scale = 0.5


def to_tiles(field):
    blocks = field.reshape(GX, N_COL, GY // N_COL, GZ, F)
    blocks = jnp.transpose(blocks, (1, 0, 2, 3, 4))
    return blocks.reshape(COL_TILES, TILE, F)


def from_tiles(tiles):
    blocks = tiles.reshape(N_COL, GX, GY // N_COL, GZ, F)
    blocks = jnp.transpose(blocks, (1, 0, 2, 3, 4))
    return blocks.reshape(GX, GY, GZ, F)


def flux(delta):
    scaled = delta / edge_scale
    return delta / (1.0 + scaled * scaled)


def diffuse_padded(padded):
    center = padded[1:-1, 1:-1, 1:-1]
    total = flux(padded[2:, 1:-1, 1:-1] - center) + flux(padded[:-2, 1:-1, 1:-1] - center)
    total = total + flux(padded[1:-1, 2:, 1:-1] - center) + flux(padded[1:-1, :-2, 1:-1] - center)
    total = total + flux(padded[1:-1, 1:-1, 2:] - center) + flux(padded[1:-1, 1:-1, :-2] - center)
    return center + diff_rate * total


def reference(image, u_factors, v_factors, ranks, measured):
    xtiles = to_tiles(image.astype(jnp.bfloat16)).astype(jnp.float32)
    mask = (jnp.arange(RMAX, dtype=jnp.int32)[None, None, :] < ranks[:, :, None]).astype(jnp.float32)

    def forward(items):
        u_row, v_row, m_row = items
        coef = jnp.einsum('jkr,jkf->jrf', v_row.astype(jnp.float32), xtiles) * m_row[:, :, None]
        coef = coef.astype(jnp.bfloat16).astype(jnp.float32)
        return jnp.einsum('jkr,jrf->kf', u_row.astype(jnp.float32), coef)

    predicted = lax.map(forward, (u_factors, v_factors, mask))
    resid = (predicted.reshape(SAMPLES, F) - measured.astype(jnp.float32)).astype(jnp.bfloat16)
    resid = resid.reshape(ROW_TILES, TILE, F).astype(jnp.float32)

    def adjoint(carry, items):
        u_row, v_row, m_row, r_row = items
        back = jnp.einsum('jkr,kf->jrf', u_row.astype(jnp.float32), r_row) * m_row[:, :, None]
        back = back.astype(jnp.bfloat16).astype(jnp.float32)
        return carry + jnp.einsum('jkr,jrf->jkf', v_row.astype(jnp.float32), back), None

    start = jnp.zeros((COL_TILES, TILE, F), jnp.float32)
    gradient, unused = lax.scan(adjoint, start, (u_factors, v_factors, mask, resid))
    moved = image - from_tiles(gradient)
    for step in range(2):
        moved = diffuse_padded(jnp.pad(moved, ((1, 1), (1, 1), (1, 1), (0, 0))))
    return moved
```

```python
import jax
import jax.numpy as jnp
from jax import lax
from jax.experimental import pallas as pl
from jax.experimental.pallas import tpu as pltpu
from jax.sharding import PartitionSpec as P

MESH = pl.DeviceIdType.MESH
NT = (((1,), (1,)), ((), ()))
BF = jnp.bfloat16
F32 = jnp.float32

LAG_RELAY, LAG_SUM, LAG_RESID, LAG_SPREAD, LAG_FORWARD, LAG_BACK = 2, 4, 6, 8, 10, 12


class Copy:
    def __init__(self, src, dst, ss, rs, dev):
        self.parts = (src, dst, ss, rs, dev)

    def made(self):
        src, dst, (ss, si), (rs, ri), dev = self.parts
        return pltpu.make_async_remote_copy(
            src_ref=at(src), dst_ref=at(dst), send_sem=ss.at[si], recv_sem=rs.at[ri], device_id=dev, device_id_type=MESH)

    def start(self):
        self.made().start()

    def wait_recv(self):
        self.made().wait_recv()

    def wait_send(self):
        self.made().wait_send()


def at(place):
    if not isinstance(place, tuple):
        return place
    ref, *index = place
    return ref.at[tuple(index)]


def flux(d):
    return d / (1.0 + 4.0 * (d * d))


def kernel(
    img_hbm, u_hbm, v_hbm, ranks, meas_hbm, out,
    img, u, v, mb, mt, xt, coef,
    ps, d2, qb, r1, sums, ph2, r2, rt,
    grad, cs, cr, zs, zd, zr, moved, m16, hr, hc, hx, s1,
    lsem, ax_s, ax_r, ex_s, ex_r, gc_s, gc_r, gz_s, gz_r, hs_s, hs_r,
):
    n_i = u.shape[0]
    r = lax.axis_index("row")
    c = lax.axis_index("col")
    z, h = r // 2, r % 2
    y, x = c // 4, c % 4
    zp, zm, zf = (z + 1) % 4, (z + 3) % 4, (z + 2) % 4
    order = (z, zm, zp, zf)

    img_copy = pltpu.make_async_copy(img_hbm, img, lsem.at[0])
    img_copy.start()
    v_copies = [pltpu.make_async_copy(v_hbm.at[:, order[k]], v.at[:, k], lsem.at[1 + k]) for k in range(4)]
    u_copies = [pltpu.make_async_copy(u_hbm.at[:, order[k]], u.at[:, k], lsem.at[5 + k]) for k in range(4)]
    m_copies = [pltpu.make_async_copy(meas_hbm.at[:, 0, x], mb.at[0], lsem.at[9]),
                pltpu.make_async_copy(meas_hbm.at[:, 1, y], mb.at[1], lsem.at[10])]

    def at_z(zz, hh=h):
        return (zz * 2 + hh, c)

    sibling = at_z(z, 1 - h)
    rp, rm = (r + 1) % 8, (r + 7) % 8
    cp, cm = (c + 1) % 16, (c + 15) % 16

    def along_x(pos):
        return (r, y * 4 + pos)

    def along_y(pos):
        return (r, pos * 4 + x)

    peers = [sibling, at_z(zp), at_z(zm)]
    peers += [along_x((x + d) % 4) for d in (1, 2, 3)] + [along_y((y + d) % 4) for d in (1, 2, 3)]
    peers += [(rp, c), (rm, c), (r, cp), (r, cm), (rp, cp), (rp, cm), (rm, cp), (rm, cm)]
    barrier = pltpu.get_barrier_semaphore()
    for peer in peers:
        pl.semaphore_signal(barrier, inc=1, device_id=peer, device_id_type=MESH)

    img_copy.wait()
    v_copies[0].start()
    for k in (1, 2, 3):
        v_copies[k].start()
    for m in m_copies:
        m.start()
    for k in range(4):
        u_copies[k].start()
    xt[r] = img[...].T.astype(BF)
    pl.semaphore_wait(barrier, len(peers))

    lo, hi = pl.ds(0, 64), pl.ds(64, 64)

    def xcopy(i, blk, part, dev):
        ref = (xt, blk) if part is None else (xt, blk, part)
        return Copy(ref, ref, (ax_s, i), (ax_r, i), dev)

    b0, bm, bp, bf = r, zm * 2 + h, zp * 2 + h, zf * 2 + h
    o0, om, op, of = z * 2 + 1 - h, zm * 2 + 1 - h, zp * 2 + 1 - h, zf * 2 + 1 - h
    out_x = [
        xcopy(0, b0, None, sibling),
        xcopy(1, b0, lo, at_z(zp)), xcopy(2, b0, hi, at_z(zm)), xcopy(3, b0, hi, at_z(zp)), xcopy(4, b0, lo, at_z(zm)),
        xcopy(5, bm, lo, at_z(zp)), xcopy(6, bp, hi, at_z(zm)),
        xcopy(7, bm, lo, sibling), xcopy(8, bp, hi, sibling), xcopy(9, bm, hi, sibling), xcopy(10, bp, lo, sibling),
        xcopy(11, bf, lo, sibling), xcopy(12, bf, hi, sibling),
    ]
    in_x = [
        xcopy(0, o0, None, sibling),
        xcopy(1, bm, lo, sibling), xcopy(2, bp, hi, sibling), xcopy(3, bm, hi, sibling), xcopy(4, bp, lo, sibling),
        xcopy(5, bf, lo, sibling), xcopy(6, bf, hi, sibling),
        xcopy(7, om, lo, sibling), xcopy(8, op, hi, sibling), xcopy(9, om, hi, sibling), xcopy(10, op, lo, sibling),
        xcopy(11, of, lo, sibling), xcopy(12, of, hi, sibling),
    ]
    for i in (1, 2, 0, 3, 4):
        out_x[i].start()

    lane = lax.broadcasted_iota(jnp.int32, (128, 256), 1)

    def masked(value, i, k):
        return jnp.where(lane < ranks[order[k], i], value, 0.0).astype(BF)

    def coefs(k):
        v_copies[k].wait()

        def one(i, _):
            j = order[k]
            xj = jnp.concatenate([xt[2 * j], xt[2 * j + 1]], axis=1)
            coef[i, k] = masked(jnp.dot(xj, v[i, k], preferred_element_type=F32), i, k)
            return 0

        lax.fori_loop(0, n_i, one, 0)

    in_x[0].wait_recv()
    coefs(0)
    in_x[1].wait_recv()
    out_x[5].start()
    out_x[7].start()
    in_x[2].wait_recv()
    out_x[6].start()
    out_x[8].start()
    for m in m_copies:
        m.wait()

    def turn(i, _):
        for ax in (0, 1):
            mt[i, ax] = mb[ax, i].astype(F32).T
        return 0

    lax.fori_loop(0, n_i, turn, 0)
    in_x[3].wait_recv()
    out_x[9].start()
    in_x[4].wait_recv()
    out_x[10].start()
    in_x[7].wait_recv()
    in_x[9].wait_recv()
    coefs(1)
    in_x[8].wait_recv()
    in_x[10].wait_recv()
    coefs(2)
    in_x[5].wait_recv()
    out_x[11].start()
    in_x[6].wait_recv()
    out_x[12].start()
    in_x[11].wait_recv()
    in_x[12].wait_recv()
    coefs(3)
    for k in range(4):
        u_copies[k].wait()

    axes = (
        (0, x, along_x, y, along_y),
        (4, y, along_y, x, along_x),
    )

    def exch(i, ax):
        base, p, dev1, s, dev2 = axes[ax]
        pp, pm, pf = (p + 1) % 4, (p + 3) % 4, (p + 2) % 4

        def cpy(n, src, dst, dev):
            return Copy(src, dst, (ex_s, (i, ax, n)), (ex_r, (i, ax, n)), dev)

        def piece(pos):
            return pl.ds(pl.multiple_of(pos * 32, 32), 32)

        own = (rt, i, base + p)
        sends = [
            cpy(0, (ps, i, base + pf, lo), (d2, i, ax, 0), dev1(pp)),
            cpy(1, (ps, i, base + pf, hi), (d2, i, ax, 1), dev1(pm)),
            cpy(2, (ps, i, base + pp, hi), (r1, i, ax, 0, hi), dev1(pp)),
            cpy(3, (ps, i, base + pm, lo), (r1, i, ax, 1, lo), dev1(pm)),
            cpy(4, (qb, i, ax, 0), (r1, i, ax, 0, lo), dev1(pp)),
            cpy(5, (qb, i, ax, 1), (r1, i, ax, 1, hi), dev1(pm)),
        ]
        for d in (1, 2, 3):
            sends.append(cpy(5 + d, (ph2, i, ax, piece((s + d) % 4)), (r2, i, ax, d - 1), dev2((s + d) % 4)))
        for d in (1, 2, 3):
            sends.append(cpy(8 + d, own + (piece(s),), own + (piece(s),), dev2((s + d) % 4)))
        sends += [
            cpy(12, own + (lo,), own + (lo,), dev1(pp)),
            cpy(13, own + (hi,), own + (hi,), dev1(pm)),
            cpy(14, own + (hi,), own + (hi,), dev1(pp)),
            cpy(15, own + (lo,), own + (lo,), dev1(pm)),
            cpy(16, (rt, i, base + pm, lo), (rt, i, base + pm, lo), dev1(pp)),
            cpy(17, (rt, i, base + pp, hi), (rt, i, base + pp, hi), dev1(pm)),
        ]
        lands = [(d2, i, ax, 0), (d2, i, ax, 1), (r1, i, ax, 0, hi), (r1, i, ax, 1, lo), (r1, i, ax, 0, lo), (r1, i, ax, 1, hi)]
        lands += [(r2, i, ax, d - 1) for d in (1, 2, 3)]
        lands += [own + (piece((s + 4 - d) % 4),) for d in (1, 2, 3)]
        lands += [(rt, i, base + pm, lo), (rt, i, base + pp, hi), (rt, i, base + pm, hi), (rt, i, base + pp, lo),
                  (rt, i, base + pf, lo), (rt, i, base + pf, hi)]

        def wait(*ns):
            for n in ns:
                cpy(n, lands[n], lands[n], dev1(pp)).wait_recv()

        return sends, wait, base, p, pp, pm, s, piece

    def stage_pred(i):
        cf = [coef[i, k] for k in range(4)]
        for q in range(4):
            rows = slice(256 * q, 256 * q + 256)
            total = lax.dot_general(cf[0], u[i, 0, rows], NT, preferred_element_type=F32)
            for k in (1, 2, 3):
                total += lax.dot_general(cf[k], u[i, k, rows], NT, preferred_element_type=F32)
            ps[i, 2 * q] = total[:, :128].astype(BF)
            ps[i, 2 * q + 1] = total[:, 128:].astype(BF)
        both = [exch(i, ax)[0] for ax in (0, 1)]
        for n in range(4):
            for sends in both:
                sends[n].start()

    def stage_relay(i):
        for ax in (0, 1):
            sends, wait, base, p, pp, pm, s, piece = exch(i, ax)
            wait(0)
            qb[i, ax, 0] = (ps[i, base + pp, :64].astype(F32) + d2[i, ax, 0].astype(F32)).astype(BF)
            sends[4].start()
            wait(1)
            qb[i, ax, 1] = (ps[i, base + pm, 64:].astype(F32) + d2[i, ax, 1].astype(F32)).astype(BF)
            sends[5].start()

    def stage_sum(i):
        for ax in (0, 1):
            sends, wait, base, p, pp, pm, s, piece = exch(i, ax)
            wait(2, 3, 4, 5)
            total = ps[i, base + p].astype(F32) + r1[i, ax, 0].astype(F32) + r1[i, ax, 1].astype(F32)
            sums[i, ax] = total
            ph2[i, ax] = total.astype(BF)
            for n in (7, 6, 8):
                sends[n].start()

    def stage_resid(i):
        for ax in (0, 1):
            sends, wait, base, p, pp, pm, s, piece = exch(i, ax)
            wait(6, 7, 8)
            total = sums[i, ax, piece(s)]
            for d in range(3):
                total += r2[i, ax, d].astype(F32)
            rt[i, base + p, piece(s)] = (total - mt[i, ax, piece(s)]).astype(BF)
            for n in (10, 9, 11):
                sends[n].start()

    def stage_spread(i):
        for ax in (0, 1):
            sends, wait, base, p, pp, pm, s, piece = exch(i, ax)
            wait(9, 10, 11)
            for n in (12, 13, 14, 15):
                sends[n].start()

    def stage_forward(i):
        for ax in (0, 1):
            sends, wait, *_ = exch(i, ax)
            wait(12)
            sends[16].start()
            wait(13)
            sends[17].start()

    def stage_wait(i):
        for ax in (0, 1):
            exch(i, ax)[1](14, 15, 16, 17)

    def back(i, k):
        res = jnp.concatenate([rt[i, q] for q in range(8)], axis=1)
        return masked(jnp.dot(res, u[i, k], preferred_element_type=F32), i, k)

    def stage_back(i):
        stage_wait(i)
        bk = [back(i, k) for k in range(4)]
        for k in range(4):
            for q in range(4):
                rows = slice(256 * q, 256 * q + 256)
                grad[k, :, rows] += lax.dot_general(bk[k], v[i, k, rows], NT, preferred_element_type=F32)

    grad[...] = jnp.zeros_like(grad)

    def slot(t, _):
        def run(lag, last, stage):
            i = t - lag
            pl.when(jnp.logical_and(i >= 0, i < last))(lambda: stage(i))

        run(0, n_i, stage_pred)
        run(LAG_FORWARD, n_i, stage_forward)
        run(LAG_SPREAD, n_i, stage_spread)
        run(LAG_RESID, n_i, stage_resid)
        run(LAG_SUM, n_i, stage_sum)
        run(LAG_RELAY, n_i, stage_relay)
        run(LAG_BACK, n_i - 1, stage_back)
        return 0

    lax.fori_loop(0, n_i + LAG_FORWARD, slot, 0)

    def tail(i, _):
        stage_back(i)
        return 0

    lax.fori_loop(n_i + LAG_FORWARD - LAG_BACK, n_i - 1, tail, 0)

    mine = pl.ds(pl.multiple_of(h * 512, 512), 512)
    other = pl.ds(pl.multiple_of((1 - h) * 512, 512), 512)
    last = n_i - 1
    stage_wait(last)
    core = [Copy((cs, k), (cr, k), (gc_s, k), (gc_r, k), sibling) for k in range(4)]
    for k in (3, 2, 1, 0):
        bk = back(last, k)
        for q in range(4):
            rows = slice(256 * q, 256 * q + 256)
            grad[k, :, rows] += lax.dot_general(bk, v[last, k, rows], NT, preferred_element_type=F32)
        cs[k] = grad[k, :, other].astype(BF)
        core[k].start()

    zsend = [
        Copy((zs, 3, lo), (zd, 0), (gz_s, 0), (gz_r, 0), at_z(zp)),
        Copy((zs, 3, hi), (zd, 1), (gz_s, 1), (gz_r, 1), at_z(zm)),
        Copy((zs, 2, hi), (zr, 0, hi), (gz_s, 2), (gz_r, 2), at_z(zp)),
        Copy((zs, 1, lo), (zr, 1, lo), (gz_s, 3), (gz_r, 3), at_z(zm)),
        Copy((zs, 2, lo), (zr, 0, lo), (gz_s, 4), (gz_r, 4), at_z(zp)),
        Copy((zs, 1, hi), (zr, 1, hi), (gz_s, 5), (gz_r, 5), at_z(zm)),
    ]
    core[3].wait_recv()
    zs[3] = (grad[3, :, mine] + cr[3].astype(F32)).astype(BF)
    zsend[0].start()
    zsend[1].start()
    core[2].wait_recv()
    zs[2, 64:] = (grad[2, 64:, mine] + cr[2, 64:].astype(F32)).astype(BF)
    zsend[2].start()
    core[1].wait_recv()
    zs[1, :64] = (grad[1, :64, mine] + cr[1, :64].astype(F32)).astype(BF)
    zsend[3].start()
    zsend[0].wait_recv()
    zs[2, :64] = (grad[2, :64, mine] + cr[2, :64].astype(F32) + zd[0].astype(F32)).astype(BF)
    zsend[4].start()
    zsend[1].wait_recv()
    zs[1, 64:] = (grad[1, 64:, mine] + cr[1, 64:].astype(F32) + zd[1].astype(F32)).astype(BF)
    zsend[5].start()
    core[0].wait_recv()
    grad[0, :, mine] += cr[0].astype(F32)
    for n in (2, 3, 4, 5):
        zsend[n].wait_recv()
    total = grad[0, :, mine] + zr[0].astype(F32) + zr[1].astype(F32)
    new = (img[...] - total.T).reshape(8, 64, 128)
    moved[...] = new
    m16[...] = new.astype(BF)

    hsend = [
        Copy(m16, (hc, 0), (hs_s, 0), (hs_r, 0), (r, cp)),
        Copy(m16, (hc, 1), (hs_s, 1), (hs_r, 1), (r, cm)),
        Copy((m16, pl.ds(4, 4)), (hr, 0), (hs_s, 2), (hs_r, 2), (rp, c)),
        Copy((m16, pl.ds(0, 4)), (hr, 1), (hs_s, 3), (hs_r, 3), (rm, c)),
        Copy((m16, 7), (hx, 0), (hs_s, 4), (hs_r, 4), (rp, cp)),
        Copy((m16, 6), (hx, 1), (hs_s, 5), (hs_r, 5), (rp, cm)),
        Copy((m16, 1), (hx, 2), (hs_s, 6), (hs_r, 6), (rm, cp)),
        Copy((m16, 0), (hx, 3), (hs_s, 7), (hs_r, 7), (rm, cm)),
    ]
    for n in (4, 5, 6, 7, 0, 1, 2, 3):
        hsend[n].start()

    for cpy in out_x + core + zsend:
        cpy.wait_send()

    def left(i, _):
        for ax in (0, 1):
            for cpy in exch(i, ax)[0]:
                cpy.wait_send()
        return 0

    lax.fori_loop(0, n_i, left, 0)
    for n in range(8):
        hsend[n].wait_recv()

    has = {-1: r > 0, 4: r < 7}
    hasc = {-1: c > 0, 2: c < 15}
    zrow = lax.broadcasted_iota(jnp.int32, (64, 128), 0)

    def inside(a, b):
        conds = []
        if a < 0 or a > 3:
            conds.append(has[-1 if a < 0 else 4])
        if b < 0 or b > 1:
            conds.append(hasc[-1 if b < 0 else 2])
        return conds

    def clip(a, b, value):
        for cond in inside(a, b):
            value = jnp.where(cond, value, 0.0)
        return value

    def first(a, b):
        if 0 <= a <= 3 and 0 <= b <= 1:
            return moved[2 * a + b]
        if 0 <= b <= 1:
            got = hr[0, 2 * (a + 2) + b] if a < 0 else hr[1, 2 * (a - 4) + b]
        elif 0 <= a <= 3:
            got = hc[0, 2 * a + b + 2] if b < 0 else hc[1, 2 * a + b - 2]
        else:
            got = hx[(0 if a < 0 else 2) + (0 if b < 0 else 1)]
        return clip(a, b, got.astype(F32))

    def second(a, b):
        if 0 <= a <= 3 and 0 <= b <= 1:
            return s1[2 * a + b]
        if 0 <= b <= 1:
            return s1[8 + b if a < 0 else 10 + b]
        return s1[12 + a if b < 0 else 16 + a]

    def diffuse(source, cells, store):
        fx, fy = {}, {}

        def edge(table, a, b, da, db):
            if (a, b) not in table:
                table[a, b] = flux(source(a + da, b + db) - source(a, b))
            return table[a, b]

        for a, b in cells:
            center = source(a, b)
            up = jnp.where(zrow == 63, 0.0, pltpu.roll(center, 63, 0))
            fz = flux(up - center)
            edge0 = flux(-center)
            down = jnp.where(zrow == 0, edge0, -pltpu.roll(fz, 1, 0))
            total = edge(fx, a, b, 1, 0) - edge(fx, a - 1, b, 1, 0) + edge(fy, a, b, 0, 1) - edge(fy, a, b - 1, 0, 1)
            total = total + fz + down
            store(a, b, center + 0.12 * total)

    def store1(a, b, value):
        slot_of = 2 * a + b
        if not 0 <= a <= 3:
            slot_of = 8 + b if a < 0 else 10 + b
        elif not 0 <= b <= 1:
            slot_of = 12 + a if b < 0 else 16 + a
        s1[slot_of] = clip(a, b, value)

    def store2(a, b, value):
        out[2 * a + b] = value

    own_cells = [(a, b) for a in range(4) for b in (0, 1)]
    cells1 = [(a, b) for a in range(-1, 5) for b in range(-1, 3) if 0 <= a <= 3 or 0 <= b <= 1]
    diffuse(first, cells1, store1)
    diffuse(second, own_cells, store2)
    for n in range(8):
        hsend[n].wait_send()


def body(image, u_factors, v_factors, ranks, measured):
    row_tiles, col_tiles, tile_len, rank_max = u_factors.shape
    f = image.shape[3]
    voxels = image.shape[0] * image.shape[1] * image.shape[2]
    anywhere = pl.BlockSpec(memory_space=pl.ANY)
    n = row_tiles
    vm = pltpu.VMEM
    dma = pltpu.SemaphoreType.DMA
    new = pl.pallas_call(
        kernel,
        out_shape=jax.ShapeDtypeStruct((8, 64, f), F32),
        in_specs=[anywhere, anywhere, anywhere, pl.BlockSpec(memory_space=pltpu.SMEM), anywhere],
        out_specs=pl.BlockSpec(memory_space=pltpu.VMEM),
        scratch_shapes=[
            vm((voxels, f), F32),
            vm((n, 4, tile_len, rank_max), BF), vm((n, 4, tile_len, rank_max), BF),
            vm((2, n, 128, f), BF), vm((n, 2, f, 128), F32),
            vm((8, f, voxels), BF), vm((n, 4, f, rank_max), BF),
            vm((n, 8, f, 128), BF), vm((n, 2, 2, 64, 128), BF), vm((n, 2, 2, 64, 128), BF),
            vm((n, 2, 2, f, 128), BF), vm((n, 2, f, 128), F32), vm((n, 2, f, 128), BF),
            vm((n, 2, 3, 32, 128), BF), vm((n, 8, f, 128), BF),
            vm((4, f, tile_len), F32), vm((4, f, 512), BF), vm((4, f, 512), BF), vm((4, f, 512), BF),
            vm((2, 64, 512), BF), vm((2, f, 512), BF),
            vm((8, 64, f), F32), vm((8, 64, f), BF), vm((2, 4, 64, f), BF), vm((2, 8, 64, f), BF), vm((4, 64, f), BF),
            vm((20, 64, f), F32),
            dma((11,)), dma((13,)), dma((13,)), dma((n, 2, 18)), dma((n, 2, 18)),
            dma((4,)), dma((4,)), dma((6,)), dma((6,)), dma((8,)), dma((8,)),
        ],
        compiler_params=pltpu.CompilerParams(collective_id=0, has_side_effects=True, vmem_limit_bytes=56 << 20),
        name="step",
    )(
        image.reshape(voxels, f), u_factors, v_factors, ranks.T,
        measured.reshape(n, 2, 4, 128, f),
    )
    return new.reshape(image.shape)


def solution(mesh):
    placed = (
        P("row", "col", None, None),
        P("row", "col", None, None),
        P("row", "col", None, None),
        P("row", "col"),
        P("row", None),
    )
    return jax.shard_map(
        body, mesh=mesh, in_specs=placed, out_specs=P("row", "col", None, None), check_vma=False
    )
```

```python
import jax
import jax.numpy as jnp
from jax import lax
from jax.experimental import pallas as pl
from jax.experimental.pallas import tpu as pltpu
from jax.sharding import PartitionSpec as P

MESH = pl.DeviceIdType.MESH
NT = (((1,), (1,)), ((), ()))
BF = jnp.bfloat16
F32 = jnp.float32

ESEM = (0, 0, 1, 1, 1, 1, 2, 2, 2, 3, 3, 3, 4, 4, 5, 5, 5, 5)
XSEM = (0, 1, 2, 3, 4, 5, 6, 7, 8, 7, 8, 9, 9)
LAG_RELAY, LAG_SUM, LAG_RESID, LAG_SPREAD, LAG_FORWARD, LAG_BACK = 2, 4, 6, 8, 10, 12


class Copy:
    def __init__(self, src, dst, ss, rs, dev):
        self.parts = (src, dst, ss, rs, dev)

    def made(self):
        src, dst, ss, rs, dev = self.parts
        return pltpu.make_async_remote_copy(
            src_ref=at(src), dst_ref=at(dst), send_sem=at(ss), recv_sem=at(rs), device_id=dev, device_id_type=MESH)

    def start(self):
        self.made().start()

    def wait_recv(self):
        self.made().wait_recv()


def arrived(like, sem):
    ref = at(like)
    pltpu.make_async_copy(ref, ref, at(sem)).wait()


def at(place):
    if not isinstance(place, tuple):
        return place
    ref, *index = place
    return ref.at[tuple(index)]


def flux(d):
    return d / (1.0 + 4.0 * (d * d))


def kernel(
    img_hbm, u_hbm, v_hbm, ranks_hbm, meas_hbm, out,
    ranks, img, u, v, mb, mt, xt, coef,
    ps, d2, qb, r1, sums, ph2, r2, rt,
    grad, cs, cr, zs, zd, zr, moved, m16, hr, hc, hx, s1,
    lsem, ax_s, ax_r, ex_s, ex_r, gc_s, gc_r, gz_s, gz_r, hs_s, hs_r,
):
    n_i = u.shape[0]
    r = lax.axis_index("row")
    c = lax.axis_index("col")
    z, h = r // 2, r % 2
    y, x = c // 4, c % 4
    zp, zm, zf = (z + 1) % 4, (z + 3) % 4, (z + 2) % 4
    order = (z, zm, zp, zf)

    img_copy = pltpu.make_async_copy(img_hbm, img, lsem.at[0])
    img_copy.start()
    r_copy = pltpu.make_async_copy(ranks_hbm, ranks, lsem.at[7])
    r_copy.start()
    v_copies = [pltpu.make_async_copy(v_hbm.at[:, order[k]], v.at[:, k], lsem.at[1 + k]) for k in range(4)]
    u_copies = [pltpu.make_async_copy(u_hbm.at[:, order[k]], u.at[:, k], lsem.at[5]) for k in range(4)]
    m_copies = [pltpu.make_async_copy(meas_hbm.at[:, 0, x], mb.at[0], lsem.at[6]),
                pltpu.make_async_copy(meas_hbm.at[:, 1, y], mb.at[1], lsem.at[6])]

    def at_z(zz, hh=h):
        return (zz * 2 + hh, c)

    sibling = at_z(z, 1 - h)
    rp, rm = (r + 1) % 8, (r + 7) % 8
    cp, cm = (c + 1) % 16, (c + 15) % 16

    def along_x(pos):
        return (r, y * 4 + pos)

    def along_y(pos):
        return (r, pos * 4 + x)

    peers = [sibling, at_z(zp), at_z(zm)]
    peers += [along_x((x + d) % 4) for d in (1, 2, 3)] + [along_y((y + d) % 4) for d in (1, 2, 3)]
    peers += [(rp, c), (rm, c), (r, cp), (r, cm), (rp, cp), (rp, cm), (rm, cp), (rm, cm)]
    barrier = pltpu.get_barrier_semaphore()
    for peer in peers:
        pl.semaphore_signal(barrier, inc=1, device_id=peer, device_id_type=MESH)

    img_copy.wait()
    v_copies[0].start()
    for k in (1, 2, 3):
        v_copies[k].start()
    for m in m_copies:
        m.start()
    for k in range(4):
        u_copies[k].start()
    xt[r] = img[...].T.astype(BF)
    pl.semaphore_wait(barrier, len(peers))

    lo, hi = pl.ds(0, 64), pl.ds(64, 64)

    def xcopy(i, blk, part, dev):
        ref = (xt, blk) if part is None else (xt, blk, part)
        return Copy(ref, ref, (ax_s, 1 if i in (1, 2) else 0), (ax_r, XSEM[i]), dev)

    b0, bm, bp, bf = r, zm * 2 + h, zp * 2 + h, zf * 2 + h
    o0, om, op, of = z * 2 + 1 - h, zm * 2 + 1 - h, zp * 2 + 1 - h, zf * 2 + 1 - h
    out_x = [
        xcopy(0, b0, None, sibling),
        xcopy(1, b0, lo, at_z(zp)), xcopy(2, b0, hi, at_z(zm)), xcopy(3, b0, hi, at_z(zp)), xcopy(4, b0, lo, at_z(zm)),
        xcopy(5, bm, lo, at_z(zp)), xcopy(6, bp, hi, at_z(zm)),
        xcopy(7, bm, lo, sibling), xcopy(8, bp, hi, sibling), xcopy(9, bm, hi, sibling), xcopy(10, bp, lo, sibling),
        xcopy(11, bf, lo, sibling), xcopy(12, bf, hi, sibling),
    ]
    half = (xt, 0, lo)
    whole = (xt, 0)
    for i in (1, 2, 0):
        out_x[i].start()
    arrived(whole, (ax_s, 1))
    for i in (3, 4):
        out_x[i].start()
    r_copy.wait()

    lane = lax.broadcasted_iota(jnp.int32, (128, 256), 1)

    def masked(value, i, k):
        return jnp.where(lane < ranks[order[k], i], value, 0.0).astype(BF)

    def coefs(k):
        v_copies[k].wait()

        def one(i, _):
            j = order[k]
            xj = jnp.concatenate([xt[2 * j], xt[2 * j + 1]], axis=1)
            coef[i, k] = masked(jnp.dot(xj, v[i, k], preferred_element_type=F32), i, k)
            return 0

        lax.fori_loop(0, n_i, one, 0)

    arrived(whole, (ax_r, 0))
    coefs(0)
    arrived(half, (ax_r, 1))
    out_x[5].start()
    out_x[7].start()
    arrived(half, (ax_r, 2))
    out_x[6].start()
    out_x[8].start()
    arrived(mb, (lsem, 6))

    def turn(i, _):
        for ax in (0, 1):
            mt[i, ax] = mb[ax, i].astype(F32).T
        return 0

    lax.fori_loop(0, n_i, turn, 0)
    arrived(half, (ax_r, 3))
    out_x[9].start()
    arrived(half, (ax_r, 4))
    out_x[10].start()
    arrived(whole, (ax_r, 7))
    coefs(1)
    arrived(whole, (ax_r, 8))
    coefs(2)
    arrived(half, (ax_r, 5))
    out_x[11].start()
    arrived(half, (ax_r, 6))
    out_x[12].start()
    arrived(whole, (ax_r, 9))
    coefs(3)
    arrived(u, (lsem, 5))

    axes = (
        (0, x, along_x, y, along_y),
        (4, y, along_y, x, along_x),
    )

    def exch(i, ax):
        base, p, dev1, s, dev2 = axes[ax]
        pp, pm, pf = (p + 1) % 4, (p + 3) % 4, (p + 2) % 4

        def cpy(n, src, dst, dev):
            return Copy(src, dst, (ex_s, i), (ex_r, i, ESEM[n]), dev)

        def piece(pos):
            return pl.ds(pl.multiple_of(pos * 32, 32), 32)

        own = (rt, i, base + p)
        sends = [
            cpy(0, (ps, i, base + pf, lo), (d2, i, ax, 0), dev1(pp)),
            cpy(1, (ps, i, base + pf, hi), (d2, i, ax, 1), dev1(pm)),
            cpy(2, (ps, i, base + pp, hi), (r1, i, ax, 0, hi), dev1(pp)),
            cpy(3, (ps, i, base + pm, lo), (r1, i, ax, 1, lo), dev1(pm)),
            cpy(4, (qb, i, ax, 0), (r1, i, ax, 0, lo), dev1(pp)),
            cpy(5, (qb, i, ax, 1), (r1, i, ax, 1, hi), dev1(pm)),
        ]
        for d in (1, 2, 3):
            sends.append(cpy(5 + d, (ph2, i, ax, piece((s + d) % 4)), (r2, i, ax, d - 1), dev2((s + d) % 4)))
        for d in (1, 2, 3):
            sends.append(cpy(8 + d, own + (piece(s),), own + (piece(s),), dev2((s + d) % 4)))
        sends += [
            cpy(12, own + (lo,), own + (lo,), dev1(pp)),
            cpy(13, own + (hi,), own + (hi,), dev1(pm)),
            cpy(14, own + (hi,), own + (hi,), dev1(pp)),
            cpy(15, own + (lo,), own + (lo,), dev1(pm)),
            cpy(16, (rt, i, base + pm, lo), (rt, i, base + pm, lo), dev1(pp)),
            cpy(17, (rt, i, base + pp, hi), (rt, i, base + pp, hi), dev1(pm)),
        ]
        return sends, base, p, pp, pm, s, piece

    def stage_pred(i):
        cf = [coef[i, k] for k in range(4)]
        for q in range(4):
            rows = slice(256 * q, 256 * q + 256)
            total = lax.dot_general(cf[0], u[i, 0, rows], NT, preferred_element_type=F32)
            for k in (1, 2, 3):
                total += lax.dot_general(cf[k], u[i, k, rows], NT, preferred_element_type=F32)
            ps[i, 2 * q] = total[:, :128].astype(BF)
            ps[i, 2 * q + 1] = total[:, 128:].astype(BF)
        both = [exch(i, ax)[0] for ax in (0, 1)]
        for n in range(4):
            for sends in both:
                sends[n].start()

    def stage_relay(i):
        arrived((d2, i), (ex_r, i, 0))
        for ax in (0, 1):
            sends, base, p, pp, pm, s, piece = exch(i, ax)
            qb[i, ax, 0] = (ps[i, base + pp, :64].astype(F32) + d2[i, ax, 0].astype(F32)).astype(BF)
            sends[4].start()
            qb[i, ax, 1] = (ps[i, base + pm, 64:].astype(F32) + d2[i, ax, 1].astype(F32)).astype(BF)
            sends[5].start()

    def stage_sum(i):
        arrived((r1, i), (ex_r, i, 1))
        for ax in (0, 1):
            sends, base, p, pp, pm, s, piece = exch(i, ax)
            total = ps[i, base + p].astype(F32) + r1[i, ax, 0].astype(F32) + r1[i, ax, 1].astype(F32)
            sums[i, ax] = total
            ph2[i, ax] = total.astype(BF)
            for n in (7, 6, 8):
                sends[n].start()

    def stage_resid(i):
        arrived((r2, i), (ex_r, i, 2))
        for ax in (0, 1):
            sends, base, p, pp, pm, s, piece = exch(i, ax)
            total = sums[i, ax, piece(s)]
            for d in range(3):
                total += r2[i, ax, d].astype(F32)
            rt[i, base + p, piece(s)] = (total - mt[i, ax, piece(s)]).astype(BF)
            for n in (10, 9, 11):
                sends[n].start()

    def stage_spread(i):
        arrived((r2, i), (ex_r, i, 3))
        for ax in (0, 1):
            sends, base, p, pp, pm, s, piece = exch(i, ax)
            for n in (12, 13, 14, 15):
                sends[n].start()

    def stage_forward(i):
        arrived((d2, i), (ex_r, i, 4))
        for ax in (0, 1):
            sends = exch(i, ax)[0]
            sends[16].start()
            sends[17].start()

    def stage_wait(i):
        arrived((r1, i), (ex_r, i, 5))

    def back(i, k):
        res = jnp.concatenate([rt[i, q] for q in range(8)], axis=1)
        return masked(jnp.dot(res, u[i, k], preferred_element_type=F32), i, k)

    def stage_back(i):
        stage_wait(i)
        bk = [back(i, k) for k in range(4)]
        for k in range(4):
            for q in range(4):
                rows = slice(256 * q, 256 * q + 256)
                grad[k, :, rows] += lax.dot_general(bk[k], v[i, k, rows], NT, preferred_element_type=F32)

    grad[...] = jnp.zeros_like(grad)

    def slot(t, _):
        def run(lag, last, stage):
            i = t - lag
            pl.when(jnp.logical_and(i >= 0, i < last))(lambda: stage(i))

        run(0, n_i, stage_pred)
        run(LAG_FORWARD, n_i, stage_forward)
        run(LAG_SPREAD, n_i, stage_spread)
        run(LAG_RESID, n_i, stage_resid)
        run(LAG_SUM, n_i, stage_sum)
        run(LAG_RELAY, n_i, stage_relay)
        run(LAG_BACK, n_i - 1, stage_back)
        return 0

    lax.fori_loop(0, n_i + LAG_FORWARD, slot, 0)

    def tail(i, _):
        stage_back(i)
        return 0

    lax.fori_loop(n_i + LAG_FORWARD - LAG_BACK, n_i - 1, tail, 0)

    mine = pl.ds(pl.multiple_of(h * 512, 512), 512)
    other = pl.ds(pl.multiple_of((1 - h) * 512, 512), 512)
    last = n_i - 1
    stage_wait(last)
    core = [Copy((cs, k), (cr, k), (gc_s, 0), (gc_r, k), sibling) for k in range(4)]
    for k in (3, 2, 1, 0):
        bk = back(last, k)
        for q in range(4):
            rows = slice(256 * q, 256 * q + 256)
            grad[k, :, rows] += lax.dot_general(bk, v[last, k, rows], NT, preferred_element_type=F32)
        cs[k] = grad[k, :, other].astype(BF)
        core[k].start()

    zsend = [
        Copy((zs, 3, lo), (zd, 0), (gz_s, 0), (gz_r, 0), at_z(zp)),
        Copy((zs, 3, hi), (zd, 1), (gz_s, 0), (gz_r, 1), at_z(zm)),
        Copy((zs, 2, hi), (zr, 0, hi), (gz_s, 0), (gz_r, 2), at_z(zp)),
        Copy((zs, 1, lo), (zr, 1, lo), (gz_s, 0), (gz_r, 2), at_z(zm)),
        Copy((zs, 2, lo), (zr, 0, lo), (gz_s, 0), (gz_r, 2), at_z(zp)),
        Copy((zs, 1, hi), (zr, 1, hi), (gz_s, 0), (gz_r, 2), at_z(zm)),
    ]
    core[3].wait_recv()
    zs[3] = (grad[3, :, mine] + cr[3].astype(F32)).astype(BF)
    zsend[0].start()
    zsend[1].start()
    core[2].wait_recv()
    zs[2, 64:] = (grad[2, 64:, mine] + cr[2, 64:].astype(F32)).astype(BF)
    zsend[2].start()
    core[1].wait_recv()
    zs[1, :64] = (grad[1, :64, mine] + cr[1, :64].astype(F32)).astype(BF)
    zsend[3].start()
    zsend[0].wait_recv()
    zs[2, :64] = (grad[2, :64, mine] + cr[2, :64].astype(F32) + zd[0].astype(F32)).astype(BF)
    zsend[4].start()
    zsend[1].wait_recv()
    zs[1, 64:] = (grad[1, 64:, mine] + cr[1, 64:].astype(F32) + zd[1].astype(F32)).astype(BF)
    zsend[5].start()
    core[0].wait_recv()
    grad[0, :, mine] += cr[0].astype(F32)
    arrived(zr, (gz_r, 2))
    total = grad[0, :, mine] + zr[0].astype(F32) + zr[1].astype(F32)
    new = (img[...] - total.T).reshape(8, 64, 128)
    moved[...] = new
    m16[...] = new.astype(BF)

    hsend = [
        Copy(m16, (hc, 0), (hs_s, 0), (hs_r, 0), (r, cp)),
        Copy(m16, (hc, 1), (hs_s, 0), (hs_r, 0), (r, cm)),
        Copy((m16, pl.ds(4, 4)), (hr, 0), (hs_s, 0), (hs_r, 0), (rp, c)),
        Copy((m16, pl.ds(0, 4)), (hr, 1), (hs_s, 0), (hs_r, 0), (rm, c)),
        Copy((m16, 7), (hx, 0), (hs_s, 0), (hs_r, 0), (rp, cp)),
        Copy((m16, 6), (hx, 1), (hs_s, 0), (hs_r, 0), (rp, cm)),
        Copy((m16, 1), (hx, 2), (hs_s, 0), (hs_r, 0), (rm, cp)),
        Copy((m16, 0), (hx, 3), (hs_s, 0), (hs_r, 0), (rm, cm)),
    ]
    for n in (4, 5, 6, 7, 0, 1, 2, 3):
        hsend[n].start()

    arrived((xt, pl.ds(0, 6)), (ax_s, 0))
    arrived(cs, (gc_s, 0))
    arrived((zs, pl.ds(0, 3)), (gz_s, 0))
    for i in range(n_i):
        arrived((v, 0, 0, pl.ds(0, 960)), (ex_s, i))
    arrived((v, 0, 0, pl.ds(0, 896)), (hs_r, 0))

    has = {-1: r > 0, 4: r < 7}
    hasc = {-1: c > 0, 2: c < 15}
    zrow = lax.broadcasted_iota(jnp.int32, (64, 128), 0)

    def inside(a, b):
        conds = []
        if a < 0 or a > 3:
            conds.append(has[-1 if a < 0 else 4])
        if b < 0 or b > 1:
            conds.append(hasc[-1 if b < 0 else 2])
        return conds

    def clip(a, b, value):
        for cond in inside(a, b):
            value = jnp.where(cond, value, 0.0)
        return value

    def first(a, b):
        if 0 <= a <= 3 and 0 <= b <= 1:
            return moved[2 * a + b]
        if 0 <= b <= 1:
            got = hr[0, 2 * (a + 2) + b] if a < 0 else hr[1, 2 * (a - 4) + b]
        elif 0 <= a <= 3:
            got = hc[0, 2 * a + b + 2] if b < 0 else hc[1, 2 * a + b - 2]
        else:
            got = hx[(0 if a < 0 else 2) + (0 if b < 0 else 1)]
        return clip(a, b, got.astype(F32))

    def second(a, b):
        if 0 <= a <= 3 and 0 <= b <= 1:
            return s1[2 * a + b]
        if 0 <= b <= 1:
            return s1[8 + b if a < 0 else 10 + b]
        return s1[12 + a if b < 0 else 16 + a]

    def diffuse(source, cells, store):
        fx, fy = {}, {}

        def edge(table, a, b, da, db):
            if (a, b) not in table:
                table[a, b] = flux(source(a + da, b + db) - source(a, b))
            return table[a, b]

        for a, b in cells:
            center = source(a, b)
            up = jnp.where(zrow == 63, 0.0, pltpu.roll(center, 63, 0))
            fz = flux(up - center)
            edge0 = flux(-center)
            down = jnp.where(zrow == 0, edge0, -pltpu.roll(fz, 1, 0))
            total = edge(fx, a, b, 1, 0) - edge(fx, a - 1, b, 1, 0) + edge(fy, a, b, 0, 1) - edge(fy, a, b - 1, 0, 1)
            total = total + fz + down
            store(a, b, center + 0.12 * total)

    def store1(a, b, value):
        slot_of = 2 * a + b
        if not 0 <= a <= 3:
            slot_of = 8 + b if a < 0 else 10 + b
        elif not 0 <= b <= 1:
            slot_of = 12 + a if b < 0 else 16 + a
        s1[slot_of] = clip(a, b, value)

    def store2(a, b, value):
        out[2 * a + b] = value

    own_cells = [(a, b) for a in range(4) for b in (0, 1)]
    cells1 = [(a, b) for a in range(-1, 5) for b in range(-1, 3) if 0 <= a <= 3 or 0 <= b <= 1]
    diffuse(first, cells1, store1)
    diffuse(second, own_cells, store2)
    arrived((v, 0, 0, pl.ds(0, 896)), (hs_s, 0))


def body(image, u_factors, v_factors, ranks, measured):
    row_tiles, col_tiles, tile_len, rank_max = u_factors.shape
    f = image.shape[3]
    voxels = image.shape[0] * image.shape[1] * image.shape[2]
    anywhere = pl.BlockSpec(memory_space=pl.ANY)
    n = row_tiles
    vm = pltpu.VMEM
    dma = pltpu.SemaphoreType.DMA
    new = pl.pallas_call(
        kernel,
        out_shape=pltpu.VMEM((8, 64, f), F32),
        in_specs=[anywhere] * 5,
        out_specs=pl.BlockSpec(memory_space=pltpu.VMEM),
        scratch_shapes=[
            pltpu.SMEM((4, n), jnp.int32), vm((voxels, f), F32),
            vm((n, 4, tile_len, rank_max), BF), vm((n, 4, tile_len, rank_max), BF),
            vm((2, n, 128, f), BF), vm((n, 2, f, 128), F32),
            vm((8, f, voxels), BF), vm((n, 4, f, rank_max), BF),
            vm((n, 8, f, 128), BF), vm((n, 2, 2, 64, 128), BF), vm((n, 2, 2, 64, 128), BF),
            vm((n, 2, 2, f, 128), BF), vm((n, 2, f, 128), F32), vm((n, 2, f, 128), BF),
            vm((n, 2, 3, 32, 128), BF), vm((n, 8, f, 128), BF),
            vm((4, f, tile_len), F32), vm((4, f, 512), BF), vm((4, f, 512), BF), vm((4, f, 512), BF),
            vm((2, 64, 512), BF), vm((2, f, 512), BF),
            vm((8, 64, f), F32), vm((8, 64, f), BF), vm((2, 4, 64, f), BF), vm((2, 8, 64, f), BF), vm((4, 64, f), BF),
            vm((20, 64, f), F32),
            dma((8,)), dma((2,)), dma((10,)), dma((n,)), dma((n, 6)),
            dma((1,)), dma((4,)), dma((1,)), dma((3,)), dma((1,)), dma((1,)),
        ],
        compiler_params=pltpu.CompilerParams(collective_id=0, has_side_effects=True, vmem_limit_bytes=56 << 20),
        name="step",
    )(
        image.reshape(voxels, f), u_factors, v_factors, ranks.T,
        measured.reshape(n, 2, 4, 128, f),
    )
    return new.reshape(image.shape)


def solution(mesh):
    placed = (
        P("row", "col", None, None),
        P("row", "col", None, None),
        P("row", "col", None, None),
        P("row", "col"),
        P("row", None),
    )
    return jax.shard_map(
        body, mesh=mesh, in_specs=placed, out_specs=P("row", "col", None, None), check_vma=False
    )
```

```python
import jax
import jax.numpy as jnp
from jax import lax
from jax.experimental import pallas as pl
from jax.experimental.pallas import tpu as pltpu
from jax.sharding import PartitionSpec as P

MESH = pl.DeviceIdType.MESH
NT = (((1,), (1,)), ((), ()))
BF = jnp.bfloat16
F32 = jnp.float32

XSEM = (0, 1, 2, 3, 4, 5, 6, 7, 8, 7, 8, 9, 9)
GROUPS = tuple((i, 1) for i in range(5))


class Copy:
    def __init__(self, src, dst, ss, rs, dev):
        self.parts = (src, dst, ss, rs, dev)

    def made(self):
        src, dst, ss, rs, dev = self.parts
        return pltpu.make_async_remote_copy(
            src_ref=at(src), dst_ref=at(dst), send_sem=at(ss), recv_sem=at(rs), device_id=dev, device_id_type=MESH)

    def start(self):
        self.made().start()

    def wait_recv(self):
        self.made().wait_recv()


def arrived(like, sem):
    ref = at(like)
    pltpu.make_async_copy(ref, ref, at(sem)).wait()


def at(place):
    if not isinstance(place, tuple):
        return place
    ref, *index = place
    return ref.at[tuple(index)]


def flux(d):
    return d / (1.0 + 4.0 * (d * d))


def kernel(
    img_hbm, u_hbm, v_hbm, ranks_hbm, meas_hbm, out,
    ranks, img, u, v, mb, mt, xt, coef,
    ps, kept, r1, sums, ph2, r2, rt,
    grad, cs, cr, zs, zd, zr, moved, m16, hr, hc, hx, s1,
    lsem, ax_s, ax_r, ex_s, ex_r, gc_s, gc_r, gz_s, gz_r, hs_s, hs_r, ready,
):
    n_i = u.shape[0]
    r = lax.axis_index("row")
    c = lax.axis_index("col")
    z, h = r // 2, r % 2
    y, x = c // 4, c % 4
    zp, zm, zf = (z + 1) % 4, (z + 3) % 4, (z + 2) % 4
    order = (z, zm, zp, zf)

    img_copy = pltpu.make_async_copy(img_hbm, img, lsem.at[0])
    img_copy.start()
    r_copy = pltpu.make_async_copy(ranks_hbm, ranks, lsem.at[7])
    r_copy.start()
    v_copies = [pltpu.make_async_copy(v_hbm.at[:, order[k]], v.at[:, k], lsem.at[1 + k]) for k in range(4)]
    u_copies = [pltpu.make_async_copy(u_hbm.at[:, order[k]], u.at[:, k], lsem.at[5]) for k in range(4)]
    m_copies = [pltpu.make_async_copy(meas_hbm.at[:, 0, x], mb.at[0], lsem.at[6]),
                pltpu.make_async_copy(meas_hbm.at[:, 1, y], mb.at[1], lsem.at[6])]

    def at_z(zz, hh=h):
        return (zz * 2 + hh, c)

    sibling = at_z(z, 1 - h)
    rp, rm = (r + 1) % 8, (r + 7) % 8
    cp, cm = (c + 1) % 16, (c + 15) % 16

    def along_x(pos):
        return (r, y * 4 + pos)

    def along_y(pos):
        return (r, pos * 4 + x)

    sides = [along_x((x + 1) % 4), along_x((x + 3) % 4), along_y((y + 1) % 4), along_y((y + 3) % 4)]
    peers = [sibling, at_z(zp), at_z(zm)] + sides
    barrier = pltpu.get_barrier_semaphore()
    for peer in peers:
        pl.semaphore_signal(barrier, inc=1, device_id=peer, device_id_type=MESH)

    img_copy.wait()
    v_copies[0].start()
    for k in (1, 2, 3):
        v_copies[k].start()
    for m in m_copies:
        m.start()
    for k in range(4):
        u_copies[k].start()
    xt[r] = img[...].T.astype(BF)
    pl.semaphore_wait(barrier, len(peers))
    for peer in sides:
        pl.semaphore_signal(ready, inc=1, device_id=peer, device_id_type=MESH)

    lo, hi = pl.ds(0, 64), pl.ds(64, 64)

    def xcopy(i, blk, part, dev):
        ref = (xt, blk) if part is None else (xt, blk, part)
        return Copy(ref, ref, (ax_s, 1 if i in (1, 2) else 0), (ax_r, XSEM[i]), dev)

    b0, bm, bp, bf = r, zm * 2 + h, zp * 2 + h, zf * 2 + h
    o0, om, op, of = z * 2 + 1 - h, zm * 2 + 1 - h, zp * 2 + 1 - h, zf * 2 + 1 - h
    out_x = [
        xcopy(0, b0, None, sibling),
        xcopy(1, b0, lo, at_z(zp)), xcopy(2, b0, hi, at_z(zm)), xcopy(3, b0, hi, at_z(zp)), xcopy(4, b0, lo, at_z(zm)),
        xcopy(5, bm, lo, at_z(zp)), xcopy(6, bp, hi, at_z(zm)),
        xcopy(7, bm, lo, sibling), xcopy(8, bp, hi, sibling), xcopy(9, bm, hi, sibling), xcopy(10, bp, lo, sibling),
        xcopy(11, bf, lo, sibling), xcopy(12, bf, hi, sibling),
    ]
    half = (xt, 0, lo)
    whole = (xt, 0)
    for i in (1, 2, 0):
        out_x[i].start()
    arrived(whole, (ax_s, 1))
    for i in (3, 4):
        out_x[i].start()
    r_copy.wait()

    lane = lax.broadcasted_iota(jnp.int32, (128, 256), 1)

    def masked(value, i, k):
        return jnp.where(lane < ranks[order[k], i], value, 0.0).astype(BF)

    def coef_of(i, k):
        j = order[k]
        xj = jnp.concatenate([xt[2 * j], xt[2 * j + 1]], axis=1)
        return masked(jnp.dot(xj, v[i, k], preferred_element_type=F32), i, k)

    def coefs(k):
        v_copies[k].wait()

        def one(i, _):
            coef[i, k] = coef_of(i, k)
            return 0

        lax.fori_loop(0, n_i, one, 0)

    arrived(whole, (ax_r, 0))
    coefs(0)
    arrived(half, (ax_r, 1))
    out_x[5].start()
    out_x[7].start()
    arrived(half, (ax_r, 2))
    out_x[6].start()
    out_x[8].start()
    arrived(mb, (lsem, 6))

    def turn(i, _):
        for ax in (0, 1):
            mt[i, ax] = mb[ax, i].astype(F32).T
        return 0

    lax.fori_loop(0, n_i, turn, 0)
    arrived(half, (ax_r, 3))
    out_x[9].start()
    arrived(half, (ax_r, 4))
    out_x[10].start()
    arrived(whole, (ax_r, 7))
    coefs(1)
    arrived(half, (ax_r, 5))
    out_x[11].start()
    arrived(half, (ax_r, 6))
    out_x[12].start()
    arrived(whole, (ax_r, 8))
    coefs(2)
    v_copies[3].wait()
    arrived(u, (lsem, 5))
    pl.semaphore_wait(ready, len(sides))
    arrived(whole, (ax_r, 9))

    axes = ((x, along_x, y, along_y), (y, along_y, x, along_x))

    def send(g, n, src, dst, dev):
        Copy(src, dst, (ex_s, g), (ex_r, g, n), dev).start()

    def product(g):
        first, count = GROUPS[g]

        i = first
        cf = [coef[i, k] for k in range(3)] + [coef_of(i, 3)]
        tiles = pl.ds(first, count)
        for ax in (0, 1):
            p, dev1, s, dev2 = axes[ax]
            for q in (2 * ax, 2 * ax + 1):
                rows = slice(256 * q, 256 * q + 256)
                total = lax.dot_general(cf[0], u[i, 0, rows], NT, preferred_element_type=F32)
                for k in (1, 2, 3):
                    total += lax.dot_general(cf[k], u[i, k, rows], NT, preferred_element_type=F32)
                for e in (0, 1):
                    role = ((2 * q + e) % 4 - p + 4) % 4
                    part = total[:, 128 * e:128 * e + 128]
                    kept[ax, role, i] = part
                    ps[ax, role, i] = part.astype(BF)
            for d in (2, 1, 3):
                send(g, 0, (ps, ax, d, tiles), (r1, ax, d - 1, tiles), dev1((p + d) % 4))

    def total_of(g):
        first, count = GROUPS[g]
        tiles = pl.ds(first, count)
        every = slice(None)
        arrived((r1, every, every, tiles), (ex_r, g, 0))
        for ax in (0, 1):
            p, dev1, s, dev2 = axes[ax]
            for i in range(first, first + count):
                part = kept[ax, 0, i]
                for d in range(3):
                    part += r1[ax, d, i].astype(F32)
                for piece in range(4):
                    role = (piece - s + 4) % 4
                    sums[ax, role, i] = part[32 * piece:32 * piece + 32]
                    ph2[ax, role, i] = part[32 * piece:32 * piece + 32].astype(BF)
            for d in (2, 1, 3):
                send(g, 1, (ph2, ax, d, tiles), (r2, ax, d - 1, tiles), dev2((s + d) % 4))

    def resid(g):
        first, count = GROUPS[g]
        tiles = pl.ds(first, count)
        every = slice(None)
        arrived((r2, every, every, tiles), (ex_r, g, 1))
        for ax in (0, 1):
            p, dev1, s, dev2 = axes[ax]
            for i in range(first, first + count):
                part = sums[ax, 0, i]
                for d in range(3):
                    part += r2[ax, d, i].astype(F32)
                rt[ax, p, s, i] = (part - mt[i, ax, pl.ds(pl.multiple_of(s * 32, 32), 32)]).astype(BF)
            mine = (rt, ax, p, s, tiles)
            for d in (2, 1, 3):
                send(g, 2, mine, mine, dev2((s + d) % 4))

    def spread(g):
        first, count = GROUPS[g]
        tiles = pl.ds(first, count)
        every = slice(None)
        arrived((r2, every, every, tiles), (ex_r, g, 2))
        for d in (2, 1, 3):
            for ax in (0, 1):
                p, dev1, s, dev2 = axes[ax]
                mine = (rt, ax, p, slice(None), tiles)
                send(g, 3, mine, mine, dev1((p + d) % 4))

    def landed(g):
        first, count = GROUPS[g]
        every = slice(None)
        arrived((r1, every, every, pl.ds(first, count)), (ex_r, g, 3))

    def back(i, k):
        res = jnp.concatenate([rt[q // 4, q % 4, :, i].reshape(128, 128) for q in range(8)], axis=1)
        return masked(jnp.dot(res, u[i, k], preferred_element_type=F32), i, k)

    def adjoint(g, k):
        first, count = GROUPS[g]
        bk = [back(i, k) for i in range(first, first + count)]
        for q in range(4):
            rows = slice(256 * q, 256 * q + 256)
            total = grad[k, :, rows] if g else None
            for i, b in zip(range(first, first + count), bk):
                term = lax.dot_general(b, v[i, k, rows], NT, preferred_element_type=F32)
                total = term if total is None else total + term
            grad[k, :, rows] = total

    def adjoints(g):
        landed(g)
        for k in range(4):
            adjoint(g, k)

    p, t, d, a, b = product, total_of, resid, spread, adjoints
    for stage, g in (
        (p, 0), (p, 1), (p, 2), (p, 3), (t, 0), (p, 4), (t, 1), (t, 2), (d, 0), (t, 3), (d, 1), (t, 4), (d, 2), (a, 0), (d, 3), (a, 1), (d, 4), (a, 2), (b, 0), (a, 3), (a, 4), (b, 1), (b, 2), (b, 3),
    ):
        stage(g)

    mine = pl.ds(pl.multiple_of(h * 512, 512), 512)
    other = pl.ds(pl.multiple_of((1 - h) * 512, 512), 512)
    final = len(GROUPS) - 1
    landed(final)
    core = [Copy((cs, k), (cr, k), (gc_s, 0), (gc_r, k), sibling) for k in range(4)]
    for k in (3, 2, 1, 0):
        adjoint(final, k)
        cs[k] = grad[k, :, other].astype(BF)
        core[k].start()

    zsend = [
        Copy((zs, 3, lo), (zd, 0), (gz_s, 0), (gz_r, 0), at_z(zp)),
        Copy((zs, 3, hi), (zd, 1), (gz_s, 0), (gz_r, 1), at_z(zm)),
        Copy((zs, 2, hi), (zr, 0, hi), (gz_s, 0), (gz_r, 2), at_z(zp)),
        Copy((zs, 1, lo), (zr, 1, lo), (gz_s, 0), (gz_r, 2), at_z(zm)),
        Copy((zs, 2, lo), (zr, 0, lo), (gz_s, 0), (gz_r, 2), at_z(zp)),
        Copy((zs, 1, hi), (zr, 1, hi), (gz_s, 0), (gz_r, 2), at_z(zm)),
    ]
    core[3].wait_recv()
    zs[3] = (grad[3, :, mine] + cr[3].astype(F32)).astype(BF)
    zsend[0].start()
    zsend[1].start()
    core[2].wait_recv()
    zs[2, 64:] = (grad[2, 64:, mine] + cr[2, 64:].astype(F32)).astype(BF)
    zsend[2].start()
    core[1].wait_recv()
    zs[1, :64] = (grad[1, :64, mine] + cr[1, :64].astype(F32)).astype(BF)
    zsend[3].start()
    zsend[0].wait_recv()
    zs[2, :64] = (grad[2, :64, mine] + cr[2, :64].astype(F32) + zd[0].astype(F32)).astype(BF)
    zsend[4].start()
    zsend[1].wait_recv()
    zs[1, 64:] = (grad[1, 64:, mine] + cr[1, 64:].astype(F32) + zd[1].astype(F32)).astype(BF)
    zsend[5].start()
    core[0].wait_recv()
    grad[0, :, mine] += cr[0].astype(F32)
    arrived(zr, (gz_r, 2))
    total = grad[0, :, mine] + zr[0].astype(F32) + zr[1].astype(F32)
    new = (img[...] - total.T).reshape(8, 64, 128)
    moved[...] = new
    m16[...] = new.astype(BF)

    hsend = [
        Copy(m16, (hc, 0), (hs_s, 0), (hs_r, 0), (r, cp)),
        Copy(m16, (hc, 1), (hs_s, 0), (hs_r, 0), (r, cm)),
        Copy((m16, pl.ds(4, 4)), (hr, 0), (hs_s, 0), (hs_r, 0), (rp, c)),
        Copy((m16, pl.ds(0, 4)), (hr, 1), (hs_s, 0), (hs_r, 0), (rm, c)),
        Copy((m16, 7), (hx, 0), (hs_s, 0), (hs_r, 0), (rp, cp)),
        Copy((m16, 6), (hx, 1), (hs_s, 0), (hs_r, 0), (rp, cm)),
        Copy((m16, 1), (hx, 2), (hs_s, 0), (hs_r, 0), (rm, cp)),
        Copy((m16, 0), (hx, 3), (hs_s, 0), (hs_r, 0), (rm, cm)),
    ]
    for n in (4, 5, 6, 7, 0, 1, 2, 3):
        hsend[n].start()

    arrived((xt, pl.ds(0, 6)), (ax_s, 0))
    arrived(cs, (gc_s, 0))
    arrived((zs, pl.ds(0, 3)), (gz_s, 0))
    for g, (first, count) in enumerate(GROUPS):
        arrived((v, pl.ds(0, count), 0, pl.ds(0, 960)), (ex_s, g))
    arrived((v, 0, 0, pl.ds(0, 896)), (hs_r, 0))

    has = {-1: r > 0, 4: r < 7}
    hasc = {-1: c > 0, 2: c < 15}
    zrow = lax.broadcasted_iota(jnp.int32, (64, 128), 0)

    def inside(a, b):
        conds = []
        if a < 0 or a > 3:
            conds.append(has[-1 if a < 0 else 4])
        if b < 0 or b > 1:
            conds.append(hasc[-1 if b < 0 else 2])
        return conds

    def clip(a, b, value):
        for cond in inside(a, b):
            value = jnp.where(cond, value, 0.0)
        return value

    def first(a, b):
        if 0 <= a <= 3 and 0 <= b <= 1:
            return moved[2 * a + b]
        if 0 <= b <= 1:
            got = hr[0, 2 * (a + 2) + b] if a < 0 else hr[1, 2 * (a - 4) + b]
        elif 0 <= a <= 3:
            got = hc[0, 2 * a + b + 2] if b < 0 else hc[1, 2 * a + b - 2]
        else:
            got = hx[(0 if a < 0 else 2) + (0 if b < 0 else 1)]
        return clip(a, b, got.astype(F32))

    def second(a, b):
        if 0 <= a <= 3 and 0 <= b <= 1:
            return s1[2 * a + b]
        if 0 <= b <= 1:
            return s1[8 + b if a < 0 else 10 + b]
        return s1[12 + a if b < 0 else 16 + a]

    def diffuse(source, cells, store):
        fx, fy = {}, {}

        def edge(table, a, b, da, db):
            if (a, b) not in table:
                table[a, b] = flux(source(a + da, b + db) - source(a, b))
            return table[a, b]

        for a, b in cells:
            center = source(a, b)
            up = jnp.where(zrow == 63, 0.0, pltpu.roll(center, 63, 0))
            fz = flux(up - center)
            edge0 = flux(-center)
            down = jnp.where(zrow == 0, edge0, -pltpu.roll(fz, 1, 0))
            total = edge(fx, a, b, 1, 0) - edge(fx, a - 1, b, 1, 0) + edge(fy, a, b, 0, 1) - edge(fy, a, b - 1, 0, 1)
            total = total + fz + down
            store(a, b, center + 0.12 * total)

    def store1(a, b, value):
        slot_of = 2 * a + b
        if not 0 <= a <= 3:
            slot_of = 8 + b if a < 0 else 10 + b
        elif not 0 <= b <= 1:
            slot_of = 12 + a if b < 0 else 16 + a
        s1[slot_of] = clip(a, b, value)

    def store2(a, b, value):
        out[2 * a + b] = value

    own_cells = [(a, b) for a in range(4) for b in (0, 1)]
    cells1 = [(a, b) for a in range(-1, 5) for b in range(-1, 3) if 0 <= a <= 3 or 0 <= b <= 1]
    diffuse(first, cells1, store1)
    diffuse(second, own_cells, store2)
    arrived((v, 0, 0, pl.ds(0, 896)), (hs_s, 0))


def body(image, u_factors, v_factors, ranks, measured):
    row_tiles, col_tiles, tile_len, rank_max = u_factors.shape
    f = image.shape[3]
    voxels = image.shape[0] * image.shape[1] * image.shape[2]
    anywhere = pl.BlockSpec(memory_space=pl.ANY)
    n = row_tiles
    vm = pltpu.VMEM
    dma = pltpu.SemaphoreType.DMA
    new = pl.pallas_call(
        kernel,
        out_shape=pltpu.VMEM((8, 64, f), F32),
        in_specs=[anywhere] * 5,
        out_specs=pl.BlockSpec(memory_space=pltpu.VMEM),
        scratch_shapes=[
            pltpu.SMEM((4, n), jnp.int32), vm((voxels, f), F32),
            vm((n, 4, tile_len, rank_max), BF), vm((n, 4, tile_len, rank_max), BF),
            vm((2, n, 128, f), BF), vm((n, 2, f, 128), F32),
            vm((8, f, voxels), BF), vm((n, 3, f, rank_max), BF),
            vm((2, 4, n, 128, 128), BF), vm((2, 4, n, 128, 128), F32), vm((2, 3, n, 128, 128), BF),
            vm((2, 4, n, 32, 128), F32), vm((2, 4, n, 32, 128), BF), vm((2, 3, n, 32, 128), BF), vm((2, 4, 4, n, 32, 128), BF),
            vm((4, f, tile_len), F32), vm((4, f, 512), BF), vm((4, f, 512), BF), vm((4, f, 512), BF),
            vm((2, 64, 512), BF), vm((2, f, 512), BF),
            vm((8, 64, f), F32), vm((8, 64, f), BF), vm((2, 4, 64, f), BF), vm((2, 8, 64, f), BF), vm((4, 64, f), BF),
            vm((20, 64, f), F32),
            dma((8,)), dma((2,)), dma((10,)), dma((len(GROUPS),)), dma((len(GROUPS), 4)),
            dma((1,)), dma((4,)), dma((1,)), dma((3,)), dma((1,)), dma((1,)), pltpu.SemaphoreType.REGULAR,
        ],
        compiler_params=pltpu.CompilerParams(collective_id=0, has_side_effects=True, vmem_limit_bytes=56 << 20),
        name="step",
    )(
        image.reshape(voxels, f), u_factors, v_factors, ranks.T,
        measured.reshape(n, 2, 4, 128, f),
    )
    return new.reshape(image.shape)


def solution(mesh):
    placed = (
        P("row", "col", None, None),
        P("row", "col", None, None),
        P("row", "col", None, None),
        P("row", "col"),
        P("row", None),
    )
    return jax.shard_map(
        body, mesh=mesh, in_specs=placed, out_specs=P("row", "col", None, None), check_vma=False
    )
```

```python
import jax
import jax.numpy as jnp
from jax import lax
from jax.experimental import pallas as pl
from jax.experimental.pallas import tpu as pltpu
from jax.sharding import PartitionSpec as P

MESH = pl.DeviceIdType.MESH
NT = (((1,), (1,)), ((), ()))
BF = jnp.bfloat16
F32 = jnp.float32

XSEM = (0, 1, 2, 3, 4, 5, 6, 7, 8, 7, 8, 9, 9)
GROUPS = tuple((i, 1) for i in range(5))


class Copy:
    def __init__(self, src, dst, ss, rs, dev):
        self.parts = (src, dst, ss, rs, dev)

    def made(self):
        src, dst, ss, rs, dev = self.parts
        return pltpu.make_async_remote_copy(
            src_ref=at(src), dst_ref=at(dst), send_sem=at(ss), recv_sem=at(rs), device_id=dev, device_id_type=MESH)

    def start(self):
        self.made().start()

    def wait_recv(self):
        self.made().wait_recv()


def arrived(like, sem):
    ref = at(like)
    pltpu.make_async_copy(ref, ref, at(sem)).wait()


def at(place):
    if not isinstance(place, tuple):
        return place
    ref, *index = place
    return ref.at[tuple(index)]


def flux(d):
    return d / (1.0 + 4.0 * (d * d))


def kernel(
    img_hbm, u_hbm, v_hbm, ranks_hbm, meas_hbm, out,
    ranks, img, u, v, mb, mt, xt, coef,
    ps, kept, r1, sums, ph2, r2, rt,
    grad, cs, cr, zs, zd, zr, moved, m16, hr, hc, hx, s1, pre,
    lsem, ax_s, ax_r, ex_s, ex_r, gc_s, gc_r, gz_s, gz_r, hs_s, hs_r, ready,
):
    n_i = u.shape[0]
    r = lax.axis_index("row")
    c = lax.axis_index("col")
    z, h = r // 2, r % 2
    y, x = c // 4, c % 4
    zp, zm, zf = (z + 1) % 4, (z + 3) % 4, (z + 2) % 4
    order = (z, zm, zp, zf)

    img_copy = pltpu.make_async_copy(img_hbm, img, lsem.at[0])
    img_copy.start()
    r_copy = pltpu.make_async_copy(ranks_hbm, ranks, lsem.at[7])
    r_copy.start()
    v_copies = [pltpu.make_async_copy(v_hbm.at[:, order[k]], v.at[:, k], lsem.at[1 + k]) for k in range(4)]
    u_copies = [pltpu.make_async_copy(u_hbm.at[:, order[k]], u.at[:, k], lsem.at[5]) for k in range(4)]
    m_copies = [pltpu.make_async_copy(meas_hbm.at[:, 0, x], mb.at[0], lsem.at[6]),
                pltpu.make_async_copy(meas_hbm.at[:, 1, y], mb.at[1], lsem.at[6])]

    def at_z(zz, hh=h):
        return (zz * 2 + hh, c)

    sibling = at_z(z, 1 - h)
    rp, rm = (r + 1) % 8, (r + 7) % 8
    cp, cm = (c + 1) % 16, (c + 15) % 16

    def along_x(pos):
        return (r, y * 4 + pos)

    def along_y(pos):
        return (r, pos * 4 + x)

    sides = [along_x((x + 1) % 4), along_x((x + 3) % 4), along_y((y + 1) % 4), along_y((y + 3) % 4)]
    peers = [sibling, at_z(zp), at_z(zm)] + sides
    barrier = pltpu.get_barrier_semaphore()
    for peer in peers:
        pl.semaphore_signal(barrier, inc=1, device_id=peer, device_id_type=MESH)

    img_copy.wait()
    xt[r] = img[...].T.astype(BF)
    pl.semaphore_wait(barrier, len(peers))
    for peer in sides:
        pl.semaphore_signal(ready, inc=1, device_id=peer, device_id_type=MESH)

    lo, hi = pl.ds(0, 64), pl.ds(64, 64)

    def xcopy(i, blk, part, dev):
        ref = (xt, blk) if part is None else (xt, blk, part)
        return Copy(ref, ref, (ax_s, 1 if i in (1, 2) else 0), (ax_r, XSEM[i]), dev)

    b0, bm, bp, bf = r, zm * 2 + h, zp * 2 + h, zf * 2 + h
    o0, om, op, of = z * 2 + 1 - h, zm * 2 + 1 - h, zp * 2 + 1 - h, zf * 2 + 1 - h
    out_x = [
        xcopy(0, b0, None, sibling),
        xcopy(1, b0, lo, at_z(zp)), xcopy(2, b0, hi, at_z(zm)), xcopy(3, b0, hi, at_z(zp)), xcopy(4, b0, lo, at_z(zm)),
        xcopy(5, bm, lo, at_z(zp)), xcopy(6, bp, hi, at_z(zm)),
        xcopy(7, bm, lo, sibling), xcopy(8, bp, hi, sibling), xcopy(9, bm, hi, sibling), xcopy(10, bp, lo, sibling),
        xcopy(11, bf, lo, sibling), xcopy(12, bf, hi, sibling),
    ]
    half = (xt, 0, lo)
    whole = (xt, 0)
    for i in (1, 2, 0):
        out_x[i].start()
    for k in range(4):
        v_copies[k].start()
    for m in m_copies:
        m.start()
    for k in range(4):
        u_copies[k].start()
    arrived(whole, (ax_s, 1))
    for i in (3, 4):
        out_x[i].start()
    r_copy.wait()

    lane = lax.broadcasted_iota(jnp.int32, (128, 256), 1)

    def masked(value, i, k):
        return jnp.where(lane < ranks[order[k], i], value, 0.0).astype(BF)

    def coef_of(i, k):
        j = order[k]
        xj = jnp.concatenate([xt[2 * j], xt[2 * j + 1]], axis=1)
        return masked(jnp.dot(xj, v[i, k], preferred_element_type=F32), i, k)

    def coefs(k):
        v_copies[k].wait()

        def one(i, _):
            coef[i, k] = coef_of(i, k)
            return 0

        lax.fori_loop(0, n_i, one, 0)

    arrived(whole, (ax_r, 0))
    coefs(0)
    arrived(half, (ax_r, 1))
    out_x[5].start()
    out_x[7].start()
    arrived(half, (ax_r, 2))
    out_x[6].start()
    out_x[8].start()
    arrived(mb, (lsem, 6))

    def turn(i, _):
        for ax in (0, 1):
            mt[i, ax] = mb[ax, i].astype(F32).T
        return 0

    lax.fori_loop(0, n_i, turn, 0)
    arrived(half, (ax_r, 3))
    out_x[9].start()
    arrived(half, (ax_r, 4))
    out_x[10].start()
    arrived(whole, (ax_r, 7))
    coefs(1)
    arrived(half, (ax_r, 5))
    out_x[11].start()
    arrived(half, (ax_r, 6))
    out_x[12].start()
    arrived(whole, (ax_r, 8))
    coefs(2)
    v_copies[3].wait()
    arrived(u, (lsem, 5))
    pl.semaphore_wait(ready, len(sides))
    arrived(whole, (ax_r, 9))

    axes = ((x, along_x, y, along_y), (y, along_y, x, along_x))

    def send(g, n, src, dst, dev):
        Copy(src, dst, (ex_s, g), (ex_r, g, n), dev).start()

    def product(g):
        first, count = GROUPS[g]

        i = first
        cf = [coef[i, k] for k in range(3)] + [coef_of(i, 3)]
        tiles = pl.ds(first, count)
        for ax in (0, 1):
            p, dev1, s, dev2 = axes[ax]
            for q in (2 * ax, 2 * ax + 1):
                rows = slice(256 * q, 256 * q + 256)
                total = lax.dot_general(cf[0], u[i, 0, rows], NT, preferred_element_type=F32)
                for k in (1, 2, 3):
                    total += lax.dot_general(cf[k], u[i, k, rows], NT, preferred_element_type=F32)
                for e in (0, 1):
                    role = ((2 * q + e) % 4 - p + 4) % 4
                    part = total[:, 128 * e:128 * e + 128]
                    kept[ax, role, i] = part
                    ps[ax, role, i] = part.astype(BF)
            for d in (2, 1, 3):
                send(g, 0, (ps, ax, d, tiles), (r1, ax, d - 1, tiles), dev1((p + d) % 4))

    def total_of(g):
        first, count = GROUPS[g]
        tiles = pl.ds(first, count)
        every = slice(None)
        arrived((r1, every, every, tiles), (ex_r, g, 0))
        for ax in (0, 1):
            p, dev1, s, dev2 = axes[ax]
            for i in range(first, first + count):
                part = kept[ax, 0, i]
                for d in range(3):
                    part += r1[ax, d, i].astype(F32)
                for piece in range(4):
                    role = (piece - s + 4) % 4
                    sums[ax, role, i] = part[32 * piece:32 * piece + 32]
                    ph2[ax, role, i] = part[32 * piece:32 * piece + 32].astype(BF)
            for d in (2, 1, 3):
                send(g, 1, (ph2, ax, d, tiles), (r2, ax, d - 1, tiles), dev2((s + d) % 4))

    def resid(g):
        first, count = GROUPS[g]
        tiles = pl.ds(first, count)
        every = slice(None)
        arrived((r2, every, every, tiles), (ex_r, g, 1))
        for ax in (0, 1):
            p, dev1, s, dev2 = axes[ax]
            for i in range(first, first + count):
                part = sums[ax, 0, i]
                for d in range(3):
                    part += r2[ax, d, i].astype(F32)
                rt[ax, p, i, s] = (part - mt[i, ax, pl.ds(pl.multiple_of(s * 32, 32), 32)]).astype(BF)
            mine = (rt, ax, p, first, s)
            for d in (2, 1, 3):
                send(g, 2, mine, mine, dev2((s + d) % 4))

    def spread(g):
        first, count = GROUPS[g]
        tiles = pl.ds(first, count)
        every = slice(None)
        arrived((r2, every, every, tiles), (ex_r, g, 2))
        for d in (2, 1, 3):
            for ax in (0, 1):
                p, dev1, s, dev2 = axes[ax]
                mine = (rt, ax, p, first)
                send(g, 3, mine, mine, dev1((p + d) % 4))

    def landed(g):
        first, count = GROUPS[g]
        every = slice(None)
        arrived((r1, every, every, pl.ds(first, count)), (ex_r, g, 3))

    def back(i, k):
        res = jnp.concatenate([rt[q // 4, q % 4, i].reshape(128, 128) for q in range(8)], axis=1)
        return masked(jnp.dot(res, u[i, k], preferred_element_type=F32), i, k)

    def adjoint(g, k):
        first, count = GROUPS[g]
        bk = [back(i, k) for i in range(first, first + count)]
        for q in range(4):
            rows = slice(256 * q, 256 * q + 256)
            total = grad[k, :, rows] if g else None
            for i, b in zip(range(first, first + count), bk):
                term = lax.dot_general(b, v[i, k, rows], NT, preferred_element_type=F32)
                total = term if total is None else total + term
            grad[k, :, rows] = total

    def adjoints(g):
        landed(g)
        for k in range(4):
            adjoint(g, k)

    p, t, d, a, b = product, total_of, resid, spread, adjoints
    for stage, g in (
        (p, 0), (p, 1), (p, 2), (p, 3), (t, 0), (p, 4), (t, 1), (t, 2), (d, 0), (t, 3), (d, 1), (t, 4), (d, 2), (a, 0), (d, 3), (a, 1), (d, 4), (a, 2), (b, 0), (a, 3), (a, 4), (b, 1), (b, 2), (b, 3),
    ):
        stage(g)

    mine = pl.ds(pl.multiple_of(h * 512, 512), 512)
    other = pl.ds(pl.multiple_of((1 - h) * 512, 512), 512)
    final = len(GROUPS) - 1
    landed(final)
    core = [Copy((cs, k), (cr, k), (gc_s, 0), (gc_r, k), sibling) for k in range(4)]
    for k in (3, 2, 1, 0):
        adjoint(final, k)
        cs[k] = grad[k, :, other].astype(BF)
        core[k].start()

    zsend = [
        Copy((zs, 3, lo), (zd, 0), (gz_s, 0), (gz_r, 0), at_z(zp)),
        Copy((zs, 3, hi), (zd, 1), (gz_s, 0), (gz_r, 1), at_z(zm)),
        Copy((zs, 2, hi), (zr, 0, hi), (gz_s, 0), (gz_r, 2), at_z(zp)),
        Copy((zs, 1, lo), (zr, 1, lo), (gz_s, 0), (gz_r, 2), at_z(zm)),
        Copy((zs, 2, lo), (zr, 0, lo), (gz_s, 0), (gz_r, 2), at_z(zp)),
        Copy((zs, 1, hi), (zr, 1, hi), (gz_s, 0), (gz_r, 2), at_z(zm)),
    ]
    core[3].wait_recv()
    zs[3] = (grad[3, :, mine] + cr[3].astype(F32)).astype(BF)
    zsend[0].start()
    zsend[1].start()
    core[2].wait_recv()
    zs[2, 64:] = (grad[2, 64:, mine] + cr[2, 64:].astype(F32)).astype(BF)
    zsend[2].start()
    core[1].wait_recv()
    zs[1, :64] = (grad[1, :64, mine] + cr[1, :64].astype(F32)).astype(BF)
    zsend[3].start()
    zsend[0].wait_recv()
    zs[2, :64] = (grad[2, :64, mine] + cr[2, :64].astype(F32) + zd[0].astype(F32)).astype(BF)
    zsend[4].start()
    zsend[1].wait_recv()
    zs[1, 64:] = (grad[1, 64:, mine] + cr[1, 64:].astype(F32) + zd[1].astype(F32)).astype(BF)
    zsend[5].start()
    core[0].wait_recv()
    grad[0, :, mine] += cr[0].astype(F32)
    arrived(zr, (gz_r, 2))
    total = grad[0, :, mine] + zr[0].astype(F32) + zr[1].astype(F32)
    new = (img[...] - total.T).reshape(8, 64, 128)
    moved[...] = new
    m16[...] = new.astype(BF)

    hsend = [
        Copy(m16, (hc, 0), (hs_s, 0), (hs_r, 0), (r, cp)),
        Copy(m16, (hc, 1), (hs_s, 0), (hs_r, 0), (r, cm)),
        Copy((m16, pl.ds(4, 4)), (hr, 0), (hs_s, 0), (hs_r, 0), (rp, c)),
        Copy((m16, pl.ds(0, 4)), (hr, 1), (hs_s, 0), (hs_r, 0), (rm, c)),
        Copy((m16, 7), (hx, 0), (hs_s, 0), (hs_r, 0), (rp, cp)),
        Copy((m16, 6), (hx, 1), (hs_s, 0), (hs_r, 0), (rp, cm)),
        Copy((m16, 1), (hx, 2), (hs_s, 0), (hs_r, 0), (rm, cp)),
        Copy((m16, 0), (hx, 3), (hs_s, 0), (hs_r, 0), (rm, cm)),
    ]
    for n in (4, 5, 6, 7, 0, 1, 2, 3):
        hsend[n].start()

    zrow = lax.broadcasted_iota(jnp.int32, (64, 128), 0)

    def along_z(center):
        up = jnp.where(zrow == 63, 0.0, pltpu.roll(center, 63, 0))
        fz = flux(up - center)
        down = -pltpu.roll(fz, 1, 0)
        first8 = jnp.where(zrow[:8] == 0, flux(-center[:8]), down[:8])
        return fz + jnp.concatenate([first8, down[8:]], axis=0)

    for n in range(8):
        pre[n] = along_z(moved[n])

    arrived((xt, pl.ds(0, 6)), (ax_s, 0))
    arrived(cs, (gc_s, 0))
    arrived((zs, pl.ds(0, 3)), (gz_s, 0))
    for g, (first, count) in enumerate(GROUPS):
        arrived((v, pl.ds(0, count), 0, pl.ds(0, 960)), (ex_s, g))
    arrived((v, 0, 0, pl.ds(0, 896)), (hs_r, 0))

    has = {-1: r > 0, 4: r < 7}
    hasc = {-1: c > 0, 2: c < 15}

    def inside(a, b):
        conds = []
        if a < 0 or a > 3:
            conds.append(has[-1 if a < 0 else 4])
        if b < 0 or b > 1:
            conds.append(hasc[-1 if b < 0 else 2])
        return conds

    def clip(a, b, value):
        for cond in inside(a, b):
            value = jnp.where(cond, value, 0.0)
        return value

    def first(a, b):
        if 0 <= a <= 3 and 0 <= b <= 1:
            return moved[2 * a + b]
        if 0 <= b <= 1:
            got = hr[0, 2 * (a + 2) + b] if a < 0 else hr[1, 2 * (a - 4) + b]
        elif 0 <= a <= 3:
            got = hc[0, 2 * a + b + 2] if b < 0 else hc[1, 2 * a + b - 2]
        else:
            got = hx[(0 if a < 0 else 2) + (0 if b < 0 else 1)]
        return clip(a, b, got.astype(F32))

    def second(a, b):
        if 0 <= a <= 3 and 0 <= b <= 1:
            return s1[2 * a + b]
        if 0 <= b <= 1:
            return s1[8 + b if a < 0 else 10 + b]
        return s1[12 + a if b < 0 else 16 + a]

    def diffuse(source, cells, store, early):
        fx, fy = {}, {}

        def edge(table, a, b, da, db):
            if (a, b) not in table:
                table[a, b] = flux(source(a + da, b + db) - source(a, b))
            return table[a, b]

        for a, b in cells:
            center = source(a, b)
            total = edge(fx, a, b, 1, 0) - edge(fx, a - 1, b, 1, 0) + edge(fy, a, b, 0, 1) - edge(fy, a, b - 1, 0, 1)
            total = total + (pre[2 * a + b] if early and 0 <= a <= 3 and 0 <= b <= 1 else along_z(center))
            store(a, b, center + 0.12 * total)

    def store1(a, b, value):
        slot_of = 2 * a + b
        if not 0 <= a <= 3:
            slot_of = 8 + b if a < 0 else 10 + b
        elif not 0 <= b <= 1:
            slot_of = 12 + a if b < 0 else 16 + a
        s1[slot_of] = clip(a, b, value)

    def store2(a, b, value):
        out[2 * a + b] = value

    own_cells = [(a, b) for a in range(4) for b in (0, 1)]
    cells1 = [(a, b) for a in range(-1, 5) for b in range(-1, 3) if 0 <= a <= 3 or 0 <= b <= 1]
    diffuse(first, cells1, store1, True)
    diffuse(second, own_cells, store2, False)
    arrived((v, 0, 0, pl.ds(0, 896)), (hs_s, 0))


def body(image, u_factors, v_factors, ranks, measured):
    row_tiles, col_tiles, tile_len, rank_max = u_factors.shape
    f = image.shape[3]
    voxels = image.shape[0] * image.shape[1] * image.shape[2]
    anywhere = pl.BlockSpec(memory_space=pl.ANY)
    n = row_tiles
    vm = pltpu.VMEM
    dma = pltpu.SemaphoreType.DMA
    new = pl.pallas_call(
        kernel,
        out_shape=pltpu.VMEM((8, 64, f), F32),
        in_specs=[anywhere] * 5,
        out_specs=pl.BlockSpec(memory_space=pltpu.VMEM),
        scratch_shapes=[
            pltpu.SMEM((4, n), jnp.int32), vm((voxels, f), F32),
            vm((n, 4, tile_len, rank_max), BF), vm((n, 4, tile_len, rank_max), BF),
            vm((2, n, 128, f), BF), vm((n, 2, f, 128), F32),
            vm((8, f, voxels), BF), vm((n, 3, f, rank_max), BF),
            vm((2, 4, n, 128, 128), BF), vm((2, 4, n, 128, 128), F32), vm((2, 3, n, 128, 128), BF),
            vm((2, 4, n, 32, 128), F32), vm((2, 4, n, 32, 128), BF), vm((2, 3, n, 32, 128), BF), vm((2, 4, n, 4, 32, 128), BF),
            vm((4, f, tile_len), F32), vm((4, f, 512), BF), vm((4, f, 512), BF), vm((4, f, 512), BF),
            vm((2, 64, 512), BF), vm((2, f, 512), BF),
            vm((8, 64, f), F32), vm((8, 64, f), BF), vm((2, 4, 64, f), BF), vm((2, 8, 64, f), BF), vm((4, 64, f), BF),
            vm((20, 64, f), F32), vm((8, 64, f), F32),
            dma((8,)), dma((2,)), dma((10,)), dma((len(GROUPS),)), dma((len(GROUPS), 4)),
            dma((1,)), dma((4,)), dma((1,)), dma((3,)), dma((1,)), dma((1,)), pltpu.SemaphoreType.REGULAR,
        ],
        compiler_params=pltpu.CompilerParams(collective_id=0, has_side_effects=True, vmem_limit_bytes=56 << 20),
        name="step",
    )(
        image.reshape(voxels, f), u_factors, v_factors, ranks.T,
        measured.reshape(n, 2, 4, 128, f),
    )
    return new.reshape(image.shape)


def solution(mesh):
    placed = (
        P("row", "col", None, None),
        P("row", "col", None, None),
        P("row", "col", None, None),
        P("row", "col"),
        P("row", None),
    )
    return jax.shard_map(
        body, mesh=mesh, in_specs=placed, out_specs=P("row", "col", None, None), check_vma=False
    )
```

```python
import jax
import jax.numpy as jnp
from jax import lax
from jax.experimental import pallas as pl
from jax.experimental.pallas import tpu as pltpu
from jax.sharding import PartitionSpec as P

MESH = pl.DeviceIdType.MESH
NT = (((1,), (1,)), ((), ()))
BF = jnp.bfloat16
F32 = jnp.float32

XSEM = (0, 1, 2, 3, 4, 5, 6, 7, 8, 7, 8, 9, 9)
GROUPS = tuple((i, 1) for i in range(5))


class Copy:
    def __init__(self, src, dst, ss, rs, dev):
        self.parts = (src, dst, ss, rs, dev)

    def made(self):
        src, dst, ss, rs, dev = self.parts
        return pltpu.make_async_remote_copy(
            src_ref=at(src), dst_ref=at(dst), send_sem=at(ss), recv_sem=at(rs), device_id=dev, device_id_type=MESH)

    def start(self):
        self.made().start()

    def wait_recv(self):
        self.made().wait_recv()


def arrived(like, sem):
    ref = at(like)
    pltpu.make_async_copy(ref, ref, at(sem)).wait()


def at(place):
    if not isinstance(place, tuple):
        return place
    ref, *index = place
    return ref.at[tuple(index)]


def flux(d):
    return d / (1.0 + 4.0 * (d * d))


def kernel(
    img_hbm, u_hbm, v_hbm, ranks_hbm, meas_hbm, out,
    ranks, img, u, v, mb, mt, xt, coef,
    ps, kept, r1, sums, ph2, r2, rt,
    grad, cs, cr, zs, zd, zr, moved, m16, hr, hc, hx, s1, pre,
    lsem, ax_s, ax_r, ex_s, ex_r, gc_s, gc_r, gz_s, gz_r, hs_s, hs_r, ready,
):
    n_i = u.shape[0]
    r = lax.axis_index("row")
    c = lax.axis_index("col")
    z, h = r // 2, r % 2
    y, x = c // 4, c % 4
    zp, zm, zf = (z + 1) % 4, (z + 3) % 4, (z + 2) % 4
    order = (z, zm, zp, zf)

    img_copy = pltpu.make_async_copy(img_hbm, img, lsem.at[0])
    img_copy.start()
    r_copy = pltpu.make_async_copy(ranks_hbm, ranks, lsem.at[7])
    r_copy.start()
    v_copies = [pltpu.make_async_copy(v_hbm.at[:, order[k]], v.at[:, k], lsem.at[1 + k]) for k in range(4)]
    u_copies = [pltpu.make_async_copy(u_hbm.at[:, order[k]], u.at[:, k], lsem.at[5]) for k in range(4)]
    m_copies = [pltpu.make_async_copy(meas_hbm.at[:, 0, x], mb.at[0], lsem.at[6]),
                pltpu.make_async_copy(meas_hbm.at[:, 1, y], mb.at[1], lsem.at[6])]

    def at_z(zz, hh=h):
        return (zz * 2 + hh, c)

    sibling = at_z(z, 1 - h)
    rp, rm = (r + 1) % 8, (r + 7) % 8
    cp, cm = (c + 1) % 16, (c + 15) % 16

    def along_x(pos):
        return (r, y * 4 + pos)

    def along_y(pos):
        return (r, pos * 4 + x)

    sides = [along_x((x + 1) % 4), along_x((x + 3) % 4), along_y((y + 1) % 4), along_y((y + 3) % 4)]
    peers = [sibling, at_z(zp), at_z(zm)] + sides
    barrier = pltpu.get_barrier_semaphore()
    for peer in peers:
        pl.semaphore_signal(barrier, inc=1, device_id=peer, device_id_type=MESH)

    img_copy.wait()
    xt[r] = img[...].T.astype(BF)
    pl.semaphore_wait(barrier, len(peers))
    for peer in sides:
        pl.semaphore_signal(ready, inc=1, device_id=peer, device_id_type=MESH)

    lo, hi = pl.ds(0, 64), pl.ds(64, 64)

    def xcopy(i, blk, part, dev):
        ref = (xt, blk) if part is None else (xt, blk, part)
        return Copy(ref, ref, (ax_s, 1 if i in (1, 2) else 0), (ax_r, XSEM[i]), dev)

    b0, bm, bp, bf = r, zm * 2 + h, zp * 2 + h, zf * 2 + h
    o0, om, op, of = z * 2 + 1 - h, zm * 2 + 1 - h, zp * 2 + 1 - h, zf * 2 + 1 - h
    out_x = [
        xcopy(0, b0, None, sibling),
        xcopy(1, b0, lo, at_z(zp)), xcopy(2, b0, hi, at_z(zm)), xcopy(3, b0, hi, at_z(zp)), xcopy(4, b0, lo, at_z(zm)),
        xcopy(5, bm, lo, at_z(zp)), xcopy(6, bp, hi, at_z(zm)),
        xcopy(7, bm, lo, sibling), xcopy(8, bp, hi, sibling), xcopy(9, bm, hi, sibling), xcopy(10, bp, lo, sibling),
        xcopy(11, bf, lo, sibling), xcopy(12, bf, hi, sibling),
    ]
    half = (xt, 0, lo)
    whole = (xt, 0)
    for i in (1, 2, 0):
        out_x[i].start()
    for k in range(4):
        v_copies[k].start()
    for m in m_copies:
        m.start()
    for k in range(4):
        u_copies[k].start()
    arrived(whole, (ax_s, 1))
    for i in (3, 4):
        out_x[i].start()
    r_copy.wait()

    lane = lax.broadcasted_iota(jnp.int32, (128, 256), 1)

    def masked(value, i, k):
        return jnp.where(lane < ranks[order[k], i], value, 0.0).astype(BF)

    def coef_of(i, k):
        j = order[k]
        xj = jnp.concatenate([xt[2 * j], xt[2 * j + 1]], axis=1)
        return masked(jnp.dot(xj, v[i, k], preferred_element_type=F32), i, k)

    def coefs(k):
        v_copies[k].wait()

        def one(i, _):
            coef[i, k] = coef_of(i, k)
            return 0

        lax.fori_loop(0, n_i, one, 0)

    arrived(whole, (ax_r, 0))
    coefs(0)
    arrived(half, (ax_r, 1))
    out_x[5].start()
    out_x[7].start()
    arrived(half, (ax_r, 2))
    out_x[6].start()
    out_x[8].start()
    arrived(mb, (lsem, 6))

    def turn(i, _):
        for ax in (0, 1):
            mt[i, ax] = mb[ax, i].astype(F32).T
        return 0

    lax.fori_loop(0, n_i, turn, 0)
    arrived(half, (ax_r, 3))
    out_x[9].start()
    arrived(half, (ax_r, 4))
    out_x[10].start()
    arrived(whole, (ax_r, 7))
    coefs(1)
    arrived(half, (ax_r, 5))
    out_x[11].start()
    arrived(half, (ax_r, 6))
    out_x[12].start()
    arrived(whole, (ax_r, 8))
    coefs(2)
    v_copies[3].wait()
    arrived(u, (lsem, 5))
    pl.semaphore_wait(ready, len(sides))
    arrived(whole, (ax_r, 9))

    axes = ((x, along_x, y, along_y), (y, along_y, x, along_x))

    def send(g, n, src, dst, dev):
        Copy(src, dst, (ex_s, g), (ex_r, g, n), dev).start()

    def product(g):
        first, count = GROUPS[g]

        i = first
        cf = [coef[i, k] for k in range(3)] + [coef_of(i, 3)]
        tiles = pl.ds(first, count)
        for ax in (0, 1):
            p, dev1, s, dev2 = axes[ax]
            for q in (2 * ax, 2 * ax + 1):
                rows = slice(256 * q, 256 * q + 256)
                total = lax.dot_general(cf[0], u[i, 0, rows], NT, preferred_element_type=F32)
                for k in (1, 2, 3):
                    total += lax.dot_general(cf[k], u[i, k, rows], NT, preferred_element_type=F32)
                for e in (0, 1):
                    role = ((2 * q + e) % 4 - p + 4) % 4
                    part = total[:, 128 * e:128 * e + 128]
                    kept[ax, role, i] = part
                    ps[ax, role, i] = part.astype(BF)
            for d in (2, 1, 3):
                send(g, 0, (ps, ax, d, tiles), (r1, ax, d - 1, tiles), dev1((p + d) % 4))

    def total_of(g):
        first, count = GROUPS[g]
        tiles = pl.ds(first, count)
        every = slice(None)
        arrived((r1, every, every, tiles), (ex_r, g, 0))
        for ax in (0, 1):
            p, dev1, s, dev2 = axes[ax]
            for i in range(first, first + count):
                part = kept[ax, 0, i]
                for d in range(3):
                    part += r1[ax, d, i].astype(F32)
                for piece in range(4):
                    role = (piece - s + 4) % 4
                    sums[ax, role, i] = part[32 * piece:32 * piece + 32]
                    ph2[ax, role, i] = part[32 * piece:32 * piece + 32].astype(BF)
            for d in (2, 1, 3):
                send(g, 1, (ph2, ax, d, tiles), (r2, ax, d - 1, tiles), dev2((s + d) % 4))

    def resid(g):
        first, count = GROUPS[g]
        tiles = pl.ds(first, count)
        every = slice(None)
        arrived((r2, every, every, tiles), (ex_r, g, 1))
        for ax in (0, 1):
            p, dev1, s, dev2 = axes[ax]
            for i in range(first, first + count):
                part = sums[ax, 0, i]
                for d in range(3):
                    part += r2[ax, d, i].astype(F32)
                rt[ax, p, i, s] = (part - mt[i, ax, pl.ds(pl.multiple_of(s * 32, 32), 32)]).astype(BF)
            mine = (rt, ax, p, first, s)
            for d in (2, 1, 3):
                send(g, 2, mine, mine, dev2((s + d) % 4))

    def spread(g):
        first, count = GROUPS[g]
        tiles = pl.ds(first, count)
        every = slice(None)
        arrived((r2, every, every, tiles), (ex_r, g, 2))
        for d in (2, 1, 3):
            for ax in (0, 1):
                p, dev1, s, dev2 = axes[ax]
                mine = (rt, ax, p, first)
                send(g, 3, mine, mine, dev1((p + d) % 4))

    def landed(g):
        first, count = GROUPS[g]
        every = slice(None)
        arrived((r1, every, every, pl.ds(first, count)), (ex_r, g, 3))

    def back(i, k):
        res = jnp.concatenate([rt[q // 4, q % 4, i].reshape(128, 128) for q in range(8)], axis=1)
        return masked(jnp.dot(res, u[i, k], preferred_element_type=F32), i, k)

    def adjoint(g, k):
        first, count = GROUPS[g]
        bk = [back(i, k) for i in range(first, first + count)]
        for q in range(4):
            rows = slice(256 * q, 256 * q + 256)
            total = grad[k, :, rows] if g else None
            for i, b in zip(range(first, first + count), bk):
                term = lax.dot_general(b, v[i, k, rows], NT, preferred_element_type=F32)
                total = term if total is None else total + term
            grad[k, :, rows] = total

    def adjoints(g):
        landed(g)
        for k in range(4):
            adjoint(g, k)

    p, t, d, a, b = product, total_of, resid, spread, adjoints
    for stage, g in (
        (p, 0), (p, 1), (p, 2), (p, 3), (t, 0), (p, 4), (t, 1), (t, 2), (d, 0), (t, 3), (d, 1), (t, 4), (d, 2), (a, 0), (d, 3), (a, 1), (d, 4), (a, 2), (b, 0), (a, 3), (a, 4), (b, 1), (b, 2), (b, 3),
    ):
        stage(g)

    mine = pl.ds(pl.multiple_of(h * 512, 512), 512)
    other = pl.ds(pl.multiple_of((1 - h) * 512, 512), 512)
    final = len(GROUPS) - 1
    landed(final)
    core = [Copy((cs, k), (cr, k), (gc_s, 0), (gc_r, k), sibling) for k in range(4)]
    for k in (3, 2, 1, 0):
        adjoint(final, k)
        cs[k] = grad[k, :, other].astype(BF)
        core[k].start()

    zsend = [
        Copy((zs, 3, lo), (zd, 0), (gz_s, 0), (gz_r, 0), at_z(zp)),
        Copy((zs, 3, hi), (zd, 1), (gz_s, 0), (gz_r, 1), at_z(zm)),
        Copy((zs, 2, hi), (zr, 0, hi), (gz_s, 0), (gz_r, 2), at_z(zp)),
        Copy((zs, 1, lo), (zr, 1, lo), (gz_s, 0), (gz_r, 2), at_z(zm)),
        Copy((zs, 2, lo), (zr, 0, lo), (gz_s, 0), (gz_r, 2), at_z(zp)),
        Copy((zs, 1, hi), (zr, 1, hi), (gz_s, 0), (gz_r, 2), at_z(zm)),
    ]
    core[3].wait_recv()
    zs[3] = (grad[3, :, mine] + cr[3].astype(F32)).astype(BF)
    zsend[0].start()
    zsend[1].start()
    core[2].wait_recv()
    zs[2, 64:] = (grad[2, 64:, mine] + cr[2, 64:].astype(F32)).astype(BF)
    zsend[2].start()
    core[1].wait_recv()
    zs[1, :64] = (grad[1, :64, mine] + cr[1, :64].astype(F32)).astype(BF)
    zsend[3].start()
    zsend[0].wait_recv()
    zs[2, :64] = (grad[2, :64, mine] + cr[2, :64].astype(F32) + zd[0].astype(F32)).astype(BF)
    zsend[4].start()
    zsend[1].wait_recv()
    zs[1, 64:] = (grad[1, 64:, mine] + cr[1, 64:].astype(F32) + zd[1].astype(F32)).astype(BF)
    zsend[5].start()
    core[0].wait_recv()
    grad[0, :, mine] += cr[0].astype(F32)
    arrived(zr, (gz_r, 2))
    total = grad[0, :, mine] + zr[0].astype(F32) + zr[1].astype(F32)
    new = (img[...] - total.T).reshape(8, 64, 128)
    moved[...] = new
    m16[...] = new.astype(BF)

    hsend = [
        Copy(m16, (hc, 0), (hs_s, 0), (hs_r, 0), (r, cp)),
        Copy(m16, (hc, 1), (hs_s, 0), (hs_r, 0), (r, cm)),
        Copy((m16, pl.ds(4, 4)), (hr, 0), (hs_s, 0), (hs_r, 0), (rp, c)),
        Copy((m16, pl.ds(0, 4)), (hr, 1), (hs_s, 0), (hs_r, 0), (rm, c)),
        Copy((m16, 7), (hx, 0), (hs_s, 0), (hs_r, 0), (rp, cp)),
        Copy((m16, 6), (hx, 1), (hs_s, 0), (hs_r, 0), (rp, cm)),
        Copy((m16, 1), (hx, 2), (hs_s, 0), (hs_r, 0), (rm, cp)),
        Copy((m16, 0), (hx, 3), (hs_s, 0), (hs_r, 0), (rm, cm)),
    ]
    for n in (4, 5, 6, 7, 2, 3, 0, 1):
        hsend[n].start()

    zrow = lax.broadcasted_iota(jnp.int32, (64, 128), 0)

    def along_z(center):
        up = jnp.where(zrow == 63, 0.0, pltpu.roll(center, 63, 0))
        fz = flux(up - center)
        down = -pltpu.roll(fz, 1, 0)
        first8 = jnp.where(zrow[:8] == 0, flux(-center[:8]), down[:8])
        return fz + jnp.concatenate([first8, down[8:]], axis=0)

    for n in range(8):
        pre[n] = along_z(moved[n])

    arrived((xt, pl.ds(0, 6)), (ax_s, 0))
    arrived(cs, (gc_s, 0))
    arrived((zs, pl.ds(0, 3)), (gz_s, 0))
    for g, (first, count) in enumerate(GROUPS):
        arrived((v, pl.ds(0, count), 0, pl.ds(0, 960)), (ex_s, g))
    arrived((v, 0, 0, pl.ds(0, 896)), (hs_r, 0))

    has = {-1: r > 0, 4: r < 7}
    hasc = {-1: c > 0, 2: c < 15}

    def inside(a, b):
        conds = []
        if a < 0 or a > 3:
            conds.append(has[-1 if a < 0 else 4])
        if b < 0 or b > 1:
            conds.append(hasc[-1 if b < 0 else 2])
        return conds

    def clip(a, b, value):
        for cond in inside(a, b):
            value = jnp.where(cond, value, 0.0)
        return value

    def first(a, b):
        if 0 <= a <= 3 and 0 <= b <= 1:
            return moved[2 * a + b]
        if 0 <= b <= 1:
            got = hr[0, 2 * (a + 2) + b] if a < 0 else hr[1, 2 * (a - 4) + b]
        elif 0 <= a <= 3:
            got = hc[0, 2 * a + b + 2] if b < 0 else hc[1, 2 * a + b - 2]
        else:
            got = hx[(0 if a < 0 else 2) + (0 if b < 0 else 1)]
        return clip(a, b, got.astype(F32))

    def second(a, b):
        if 0 <= a <= 3 and 0 <= b <= 1:
            return s1[2 * a + b]
        if 0 <= b <= 1:
            return s1[8 + b if a < 0 else 10 + b]
        return s1[12 + a if b < 0 else 16 + a]

    def diffuse(source, cells, store, early):
        fx, fy = {}, {}

        def edge(table, a, b, da, db):
            if (a, b) not in table:
                table[a, b] = flux(source(a + da, b + db) - source(a, b))
            return table[a, b]

        for a, b in cells:
            center = source(a, b)
            total = edge(fx, a, b, 1, 0) - edge(fx, a - 1, b, 1, 0) + edge(fy, a, b, 0, 1) - edge(fy, a, b - 1, 0, 1)
            total = total + (pre[2 * a + b] if early and 0 <= a <= 3 and 0 <= b <= 1 else along_z(center))
            store(a, b, center + 0.12 * total)

    def store1(a, b, value):
        slot_of = 2 * a + b
        if not 0 <= a <= 3:
            slot_of = 8 + b if a < 0 else 10 + b
        elif not 0 <= b <= 1:
            slot_of = 12 + a if b < 0 else 16 + a
        s1[slot_of] = clip(a, b, value)

    def store2(a, b, value):
        out[2 * a + b] = value

    own_cells = [(a, b) for a in range(4) for b in (0, 1)]
    cells1 = [(a, b) for a in range(-1, 5) for b in range(-1, 3) if 0 <= a <= 3 or 0 <= b <= 1]
    diffuse(first, cells1, store1, True)
    diffuse(second, own_cells, store2, False)
    arrived((v, 0, 0, pl.ds(0, 896)), (hs_s, 0))


def body(image, u_factors, v_factors, ranks, measured):
    row_tiles, col_tiles, tile_len, rank_max = u_factors.shape
    f = image.shape[3]
    voxels = image.shape[0] * image.shape[1] * image.shape[2]
    anywhere = pl.BlockSpec(memory_space=pl.ANY)
    n = row_tiles
    vm = pltpu.VMEM
    dma = pltpu.SemaphoreType.DMA
    new = pl.pallas_call(
        kernel,
        out_shape=pltpu.VMEM((8, 64, f), F32),
        in_specs=[anywhere] * 5,
        out_specs=pl.BlockSpec(memory_space=pltpu.VMEM),
        scratch_shapes=[
            pltpu.SMEM((4, n), jnp.int32), vm((voxels, f), F32),
            vm((n, 4, tile_len, rank_max), BF), vm((n, 4, tile_len, rank_max), BF),
            vm((2, n, 128, f), BF), vm((n, 2, f, 128), F32),
            vm((8, f, voxels), BF), vm((n, 3, f, rank_max), BF),
            vm((2, 4, n, 128, 128), BF), vm((2, 4, n, 128, 128), F32), vm((2, 3, n, 128, 128), BF),
            vm((2, 4, n, 32, 128), F32), vm((2, 4, n, 32, 128), BF), vm((2, 3, n, 32, 128), BF), vm((2, 4, n, 4, 32, 128), BF),
            vm((4, f, tile_len), F32), vm((4, f, 512), BF), vm((4, f, 512), BF), vm((4, f, 512), BF),
            vm((2, 64, 512), BF), vm((2, f, 512), BF),
            vm((8, 64, f), F32), vm((8, 64, f), BF), vm((2, 4, 64, f), BF), vm((2, 8, 64, f), BF), vm((4, 64, f), BF),
            vm((20, 64, f), F32), vm((8, 64, f), F32),
            dma((8,)), dma((2,)), dma((10,)), dma((len(GROUPS),)), dma((len(GROUPS), 4)),
            dma((1,)), dma((4,)), dma((1,)), dma((3,)), dma((1,)), dma((1,)), pltpu.SemaphoreType.REGULAR,
        ],
        compiler_params=pltpu.CompilerParams(collective_id=0, has_side_effects=True, vmem_limit_bytes=56 << 20),
        name="step",
    )(
        image.reshape(voxels, f), u_factors, v_factors, ranks.T,
        measured.reshape(n, 2, 4, 128, f),
    )
    return new.reshape(image.shape)


def solution(mesh):
    placed = (
        P("row", "col", None, None),
        P("row", "col", None, None),
        P("row", "col", None, None),
        P("row", "col"),
        P("row", None),
    )
    return jax.shard_map(
        body, mesh=mesh, in_specs=placed, out_specs=P("row", "col", None, None), check_vma=False
    )
```
